256 devices in a mesh: sub: 128 (over x, z, y), section: 2 (over core).
Axes of the slice: x: 4, y: 4, z: 8, core: 2. Of those that a mesh axis runs over, the one named last changes fastest.
Arguments:
- voltages: bfloat16 [256, 2, 48, 16384], P('sub', None, None, 'section'), may hold values from -6 to 6
- delay_table: float32 [64], replicated, may hold values from -4 to 4
- delay_index: int32 [128, 48], replicated, may hold values from 0 to 63
- dm_table: float32 [32], replicated, may hold values from 0.05 to 0.4
- dm_index: int32 [128], replicated, may hold values from 0 to 31
- range_bounds: int32 [128, 2], replicated, may hold values from 0 to 256, as said below
Outputs:
- dedispersed: bfloat16 [128, 256, 2, 16384], P('sub', None, None, 'section')
The draws below stay inside these ranges and needn't reach their ends.
Inputs may be any that keep to these rules, and one draw needn't show every extreme that they name: `range_bounds`: each beam's range has 64 to 128 subbands and lies within the 256 subbands; some beam has exactly 128.
All inputs are finite; a program needn't handle non-finite values.
Results may differ from the reference program's by a relative error of at most 0.0059.
Values may be sent and summed in bfloat16 or wider, within the bound.
A program may use at most 128 MiB of HBM per device.

```python
import math
import jax
import jax.numpy as jnp
from jax import lax

STATIONS = 48
NFFT = 16384
DELAYS = 64
DMS = 32
SUBBANDS = 256
BEAMS = 128
RANGE_MAX = 128
RANGE_MIN = 64


def draw_range_bounds(key, part):
    key = jax.random.fold_in(key, 11)
    key_length, key_pick, key_start = jax.random.split(key, 3)
    lengths = jax.random.randint(key_length, (BEAMS,), RANGE_MIN, RANGE_MAX + 1)
    chosen = jax.random.randint(key_pick, (), 0, BEAMS)
    lengths = jnp.where(jnp.arange(BEAMS) == chosen, RANGE_MAX, lengths)
    starts = jax.random.randint(key_start, (BEAMS,), 0, SUBBANDS - lengths + 1)
    return jnp.stack([starts, starts + lengths], axis=1).astype(jnp.int32)


def plant(array, rng, low, largest):
    index_at = [jax.random.randint(jax.random.fold_in(rng, axis), (), 0, length) for axis, length in enumerate(array.shape)]
    longest = array.shape.index(max(array.shape))
    neighbour = index_at[:longest] + [(index_at[longest] + 1) % array.shape[longest]] + index_at[longest + 1:]
    return array.at[tuple(index_at)].set(low).at[tuple(neighbour)].set(largest)


def block_levels(stream_key, dims, cuts, low, high):
    def one(dim, shards_of):
        heights = jax.random.uniform(jax.random.fold_in(jax.random.fold_in(stream_key, 6), dim), (shards_of,), jnp.float32, low / len(cuts), high / len(cuts))
        return jnp.repeat(jnp.exp(heights), dims[dim] // shards_of).reshape((-1,) + (1,) * (len(dims) - dim - 1))

    loudness = one(*cuts[0])
    for cut in cuts[1:]:
        loudness = loudness * one(*cut)
    return loudness


def scatter_about(stream_key, extent, width, bound, cuts=(), dtype=jnp.bfloat16):
    factor_of = block_levels(stream_key, extent, cuts, -0.22, 0.18) if cuts else 1.0
    entries = jax.random.normal(stream_key, extent, jnp.float32) * width * factor_of
    return jnp.minimum(jnp.maximum(entries, -bound), bound).astype(dtype)


def setup_inputs(seed: int = 0) -> dict:
    streams_of = jax.random.split(jax.random.key(seed), 7)
    return {
        "voltages": scatter_about(streams_of[0], (SUBBANDS, 2, STATIONS, NFFT), 1.0, 6.0, ((0, 128), (3, 2))),
        "delay_table": jnp.clip(jax.random.uniform(streams_of[1], (DELAYS,), jnp.float32, -4.0, 4.0), -4.0, 4.0),
        "delay_index": plant(jax.random.randint(streams_of[2], (BEAMS, STATIONS), 0, DELAYS), jax.random.fold_in(streams_of[2], 1), 0, DELAYS - 1).astype(jnp.int32),
        "dm_table": jnp.clip(jnp.exp(jax.random.uniform(streams_of[3], (DMS,), jnp.float32, math.log(0.05), math.log(0.4))), 0.05, 0.4),
        "dm_index": plant(jax.random.randint(streams_of[4], (BEAMS,), 0, DMS), jax.random.fold_in(streams_of[4], 1), 0, DMS - 1).astype(jnp.int32),
        "range_bounds": draw_range_bounds(jax.random.fold_in(streams_of[6], 71), 0),
    }


def beam_weights(delays, frequency, stations):
    angles = (2.0 * math.pi * delays)[..., None, :] * frequency[:, None]
    scaling = 1.0 / math.sqrt(stations)
    return ((jnp.cos(angles) * scaling).astype(jnp.bfloat16), (-jnp.sin(angles) * scaling).astype(jnp.bfloat16))

def signed_bins(bin_index, length):
    return jnp.where(bin_index < length // 2, bin_index, bin_index - length).astype(jnp.float32)

def chirp_phase(dispersion, frequency, bin_values, length):
    coefficient = math.pi * dispersion / (length * (frequency * frequency * frequency))
    return coefficient.reshape(coefficient.shape + (1,) * bin_values.ndim) * (bin_values * bin_values)

def reference(voltages, delay_table, delay_index, dm_table, dm_index, range_bounds):
    subbands = voltages.shape[0]
    stations = voltages.shape[2]
    length = voltages.shape[3]
    volt_real = voltages[:, 0].astype(jnp.float32)
    volt_imag = voltages[:, 1].astype(jnp.float32)
    row_ids = jnp.arange(subbands).astype(jnp.int32)
    frequency = 1.0 + (row_ids.astype(jnp.float32) + 0.5) / subbands
    bin_values = signed_bins(jnp.arange(length).astype(jnp.int32), length)

    def one_beam(beam_index):
        delays = delay_table[delay_index[beam_index]]
        w_real, w_imag = beam_weights(delays, frequency, stations)
        w_real = w_real.astype(jnp.float32)
        w_imag = w_imag.astype(jnp.float32)
        real_part = jnp.einsum('fs,fst->ft', w_real, volt_real) - jnp.einsum('fs,fst->ft', w_imag, volt_imag)
        imag_part = jnp.einsum('fs,fst->ft', w_imag, volt_real) + jnp.einsum('fs,fst->ft', w_real, volt_imag)
        live_rows = (row_ids >= range_bounds[beam_index, 0]) & (row_ids < range_bounds[beam_index, 1])
        real_part = jnp.where(live_rows[:, None], real_part, 0.0).astype(jnp.bfloat16)
        imag_part = jnp.where(live_rows[:, None], imag_part, 0.0).astype(jnp.bfloat16)
        real_part, imag_part = lax.optimization_barrier((real_part, imag_part))
        series = real_part.astype(jnp.float32) + 1j * imag_part.astype(jnp.float32)
        spectrum = jnp.fft.fft(series, axis=-1)
        dispersion = dm_table[dm_index[beam_index]]
        phases = chirp_phase(dispersion, frequency, bin_values, length)
        filtered = spectrum * (jnp.cos(phases) + 1j * jnp.sin(phases))
        result_rows = jnp.fft.ifft(filtered, axis=-1)
        return jnp.stack([jnp.real(result_rows), jnp.imag(result_rows)], axis=1).astype(jnp.bfloat16)
    return lax.map(one_beam, jnp.arange(range_bounds.shape[0]).astype(jnp.int32))
```

```python
import functools
import math

import jax
import jax.numpy as jnp
import numpy as np
from jax import lax
from jax.experimental import pallas as pl
from jax.experimental.pallas import tpu as pltpu
from jax.sharding import PartitionSpec as P

MESH = pl.DeviceIdType.MESH
NX, NZ, NY = 4, 8, 4
LENGTH = 16384
SIDE = 128
HALF = LENGTH // 2
QUARTER = HALF // 2
CHUNKS = NZ
OFFSETS = (4, 3, 5, 2, 6, 1, 7, 0)
LANES = 256


def chunk_offset(chunk):
    step = (chunk + 1) // 2
    return lax.rem(NZ // 2 + step * (1 - 2 * lax.rem(chunk, 2)) + NZ, NZ)


def split_table(table):
    high = table.astype(jnp.bfloat16)
    low = (table - high.astype(np.float64)).astype(jnp.bfloat16)
    return np.stack([high, low])


def dft_tables():
    index = np.arange(SIDE)
    angle = 2.0 * np.pi * (np.outer(index, index) % SIDE) / SIDE
    cosine, sine = np.cos(angle), np.sin(angle)
    first = np.block([[cosine, sine], [-sine, cosine]])
    second = np.block([[cosine, -sine], [sine, cosine]])
    third = np.block([[cosine, sine], [-sine, cosine]])
    fourth = np.empty((SIDE, 2, 2 * SIDE))
    fourth[:, 0] = np.concatenate([cosine, -sine], axis=1)
    fourth[:, 1] = np.concatenate([sine, cosine], axis=1)
    fourth = fourth.reshape(2 * SIDE, 2 * SIDE) / LENGTH
    dfts = np.stack([split_table(t) for t in (first, second, third, fourth)])
    twist = 2.0 * np.pi * np.outer(index, index) / LENGTH
    bins = index[:, None] + SIDE * np.where(index < SIDE // 2, index, index - SIDE)[None, :]
    planes = np.stack([np.cos(twist), np.sin(twist), (bins * bins).astype(np.float64)])
    return dfts, planes.astype(np.float32)


def turn_coefficients():
    grid = np.cos(np.pi * (np.arange(400) + 0.5) / 400) * 0.25 + 0.25
    x = np.sqrt(grid) * 0.5 / np.sqrt(0.5)
    square = x * x
    cosine = np.polynomial.chebyshev.Chebyshev.fit(square, np.cos(2 * np.pi * x), 6, domain=[0, 0.25])
    sine = np.polynomial.chebyshev.Chebyshev.fit(
        square, np.sin(2 * np.pi * x) / x, 6, domain=[0, 0.25]
    )
    power = np.polynomial.Polynomial
    return (
        [float(v) for v in cosine.convert(kind=power).coef],
        [float(v) for v in sine.convert(kind=power).coef],
    )


def horner(coefficients, x):
    total = coefficients[-1]
    for value in coefficients[-2::-1]:
        total = total * x + value
    return total


def split(value):
    high = value.astype(jnp.bfloat16)
    return high, (value - high.astype(jnp.float32)).astype(jnp.bfloat16)


def dot(left, right):
    return jnp.dot(left, right, preferred_element_type=jnp.float32)


def kernel(
    cosine_poly,
    sine_poly,
    weights,
    voltages,
    dfts,
    planes,
    dispersion,
    gathered,
    formed,
    arrived,
    grid,
    results,
    x_send,
    x_recv,
    z_send,
    z_recv,
    own_sem,
):
    me = lax.axis_index("sub")
    core = lax.axis_index("section")
    my_x = me // (NZ * NY)
    my_z = lax.rem(me // NY, NZ)
    my_y = lax.rem(me, NY)
    plane_start = my_x * (NZ * NY)

    barrier = pltpu.get_barrier_semaphore()

    def x_partner(step):
        other_x = lax.rem(my_x - step // 2 + NX, NX)
        other_core = lax.rem(core + lax.rem(step, 2), 2)
        return other_x, other_core

    def greet_x(step, carry):
        other_x, other_core = x_partner(step)
        pl.semaphore_signal(
            barrier, inc=1, device_id=((other_x * NZ + my_z) * NY + my_y, other_core), device_id_type=MESH
        )
        return carry

    def greet_plane(step, carry):
        other = lax.rem(my_z * NY + my_y + step // 2, NZ * NY)
        other_core = lax.rem(core + lax.rem(step, 2), 2)
        pl.semaphore_signal(
            barrier, inc=1, device_id=(plane_start + other, other_core), device_id_type=MESH
        )
        return carry

    lax.fori_loop(2, 2 * NX, greet_x, 0)
    lax.fori_loop(1, 2 * NZ * NY, greet_plane, 0)

    tiles = QUARTER // LANES

    def form(step, carry):
        local = step // tiles
        start = pl.multiple_of(lax.rem(step, tiles) * LANES, LANES)
        parts = []
        for quarter in range(2):
            block = voltages[local, :, pl.ds(quarter * QUARTER + start, LANES)]
            product = dot(weights[local], block)
            parts.append(product.reshape(CHUNKS * NX, 8, LANES))
        both = jnp.concatenate(parts, axis=1).astype(jnp.bfloat16)
        formed[pl.ds(local * (CHUNKS * NX), CHUNKS * NX), :, pl.ds(start, LANES)] = both
        return carry

    lax.fori_loop(0, 2 * tiles, form, 0)

    pl.semaphore_wait(barrier, 2 * NX - 2 + 2 * NZ * NY - 1)

    def x_copy(chunk, step):
        other_x, other_core = x_partner(step)
        return pltpu.make_async_remote_copy(
            src_ref=formed.at[(other_core * CHUNKS + chunk) * NX + other_x],
            dst_ref=arrived.at[chunk, step],
            send_sem=x_send.at[chunk],
            recv_sem=x_recv.at[chunk],
            device_id=((other_x * NZ + my_z) * NY + my_y, other_core),
            device_id_type=MESH,
        )

    def own_copy(chunk):
        return pltpu.make_async_copy(
            formed.at[(core * CHUNKS + chunk) * NX + my_x], arrived.at[chunk, 0], own_sem.at[chunk]
        )

    def start_x(chunk):
        def one(step, carry):
            x_copy(chunk, step).start()
            return carry

        lax.fori_loop(1, 2 * NX, one, 0)
        own_copy(chunk).start()

    def wait_x_sent(chunk):
        pltpu.make_async_copy(
            formed.at[pl.ds(0, 2 * NX - 1)], formed.at[pl.ds(0, 2 * NX - 1)], x_send.at[chunk]
        ).wait()

    start_x(0)
    start_x(1)

    slot = (my_z * NY + my_y) * 2 + core

    def do_chunk(chunk, carry):
        pltpu.make_async_copy(
            arrived.at[chunk, pl.ds(1, 2 * NX - 1)],
            arrived.at[chunk, pl.ds(1, 2 * NX - 1)],
            x_recv.at[chunk],
        ).wait()
        own_copy(chunk).wait()

        @pl.when(chunk < CHUNKS - 2)
        def _():
            start_x(chunk + 2)

        def fold(step, carry):
            group = step // 2
            other = lax.rem(step, 2)
            half = lax.rem(core + other, 2)

            def lane_tile(index, carry):
                lanes = pl.ds(pl.multiple_of(index * SIDE, SIDE), SIDE)
                near = arrived[chunk, group * 2 + other, :, lanes].astype(jnp.float32)
                far = arrived[chunk, group * 2 + 4 + other, :, lanes].astype(jnp.float32)
                total = near + far
                row = half * (SIDE // 2) + index
                grid[group, pl.ds(row, 8, stride=SIDE), :] = total[:8]
                grid[group, pl.ds(row + QUARTER // SIDE, 8, stride=SIDE), :] = total[8:]
                return carry

            lax.fori_loop(0, QUARTER // SIDE, lane_tile, 0)
            return carry

        lax.fori_loop(0, 4, fold, 0)

        def transform(beam, carry):
            rows = pl.ds(pl.multiple_of(beam * 2 * SIDE, 2 * SIDE), 2 * SIDE)
            series = jnp.concatenate([grid[0, rows, :], grid[1, rows, :]], axis=1).astype(jnp.bfloat16)
            stage = dot(dfts[0, 0], series) + dot(dfts[0, 1], series)
            cosine, sine = planes[0], planes[1]
            turned = []
            for group in range(2):
                lanes = slice(group * SIDE, (group + 1) * SIDE)
                real, imag = stage[:SIDE, lanes], stage[SIDE:, lanes]
                turned.append(
                    jnp.concatenate([real * cosine + imag * sine, imag * cosine - real * sine], axis=1)
                )
            high, low = split(jnp.concatenate(turned, axis=0))
            stage = dot(high, dfts[1, 0]) + dot(high, dfts[1, 1]) + dot(low, dfts[1, 0])
            turned = []
            for group in range(2):
                rows_of = slice(group * SIDE, (group + 1) * SIDE)
                real, imag = stage[rows_of, :SIDE], stage[rows_of, SIDE:]
                turns = dispersion[(chunk * NY + beam) * 2 + group] * planes[2]
                turns = turns - jnp.round(turns)
                square = turns * turns
                chirp_cos = horner(cosine_poly, square)
                chirp_sin = horner(sine_poly, square) * turns
                turned.append(
                    jnp.concatenate(
                        [real * chirp_cos - imag * chirp_sin, real * chirp_sin + imag * chirp_cos], axis=1
                    )
                )
            high, low = split(jnp.concatenate(turned, axis=0))
            stage = dot(high, dfts[2, 0]) + dot(high, dfts[2, 1]) + dot(low, dfts[2, 0])
            turned = []
            for group in range(2):
                rows_of = slice(group * SIDE, (group + 1) * SIDE)
                real, imag = stage[rows_of, :SIDE], stage[rows_of, SIDE:]
                turned.append(
                    jnp.concatenate([real * cosine - imag * sine, real * sine + imag * cosine], axis=0)
                )
            high, low = split(jnp.concatenate(turned, axis=1))
            final = dot(dfts[3, 0], high) + dot(dfts[3, 1], high) + dot(dfts[3, 0], low)
            final = final.astype(jnp.bfloat16)
            for section in range(2):
                message = (chunk * NY + beam) * 2 + section
                for group in range(2):
                    parity = lax.rem(my_x + group, 2)
                    results[message, parity] = final[
                        section * SIDE : (section + 1) * SIDE, group * SIDE : (group + 1) * SIDE
                    ]
            return carry

        lax.fori_loop(0, NY, transform, 0)

        offset = chunk_offset(chunk)

        def send(step, carry):
            beam = step // 2
            section = lax.rem(step, 2)
            up = lax.rem(my_z + offset, NZ)
            down = lax.rem(my_z - offset + NZ, NZ)
            other_z = jnp.where(beam < NY // 2, up, down)
            target = plane_start + other_z * NY + beam
            message = chunk * (NY * 2) + step
            own = jnp.logical_and(target == me, section == core)

            @pl.when(own)
            def _():
                pltpu.make_async_copy(
                    results.at[message], gathered.at[:, slot], own_sem.at[CHUNKS]
                ).start()

            @pl.when(jnp.logical_not(own))
            def _():
                pltpu.make_async_remote_copy(
                    src_ref=results.at[message],
                    dst_ref=gathered.at[:, slot],
                    send_sem=z_send,
                    recv_sem=z_recv,
                    device_id=(target, section),
                    device_id_type=MESH,
                ).start()

            return carry

        lax.fori_loop(0, 2 * NY, send, 0)
        return carry

    lax.fori_loop(0, CHUNKS, do_chunk, 0)

    for chunk in range(CHUNKS):
        wait_x_sent(chunk)
    others = 2 * NZ * NY - 1
    pltpu.make_async_copy(
        results.at[0], gathered.at[:, slot], own_sem.at[CHUNKS]
    ).wait()
    pltpu.make_async_copy(results.at[pl.ds(0, others)], results.at[pl.ds(0, others)], z_send).wait()
    pltpu.make_async_copy(
        gathered.at[:, pl.ds(0, others)], gathered.at[:, pl.ds(0, others)], z_recv
    ).wait()


def in_chunk_order(values, my_z):
    grid = values.reshape((NX, NZ, 2, NY // 2) + values.shape[1:])
    doubled = jnp.concatenate([grid, grid], axis=1)
    turned = lax.dynamic_slice_in_dim(doubled, my_z, NZ, axis=1)
    up = jnp.stack([turned[:, k, 0] for k in OFFSETS])
    down = jnp.stack([turned[:, (NZ - k) % NZ, 1] for k in OFFSETS])
    return jnp.concatenate([up, down], axis=2)


def row_frequency(row_ids, subbands):
    return 1.0 + (row_ids.astype(jnp.float32) + 0.5) / subbands


def per_device(voltages, delay_table, delay_index, dm_table, dm_index, range_bounds):
    beams = delay_index.shape[0]
    stations = voltages.shape[2]
    subbands = voltages.shape[0] * lax.axis_size("sub")
    sub_index = lax.axis_index("sub")
    core = lax.axis_index("section")
    my_x = sub_index // (NZ * NY)
    my_z = lax.rem(sub_index // NY, NZ)
    own_beam = sub_index

    ordered_delay = in_chunk_order(delay_index, my_z).reshape(beams, stations)
    ordered_bounds = in_chunk_order(range_bounds, my_z).reshape(beams, 2)
    ordered_entry = in_chunk_order(dm_index, my_z)

    picked = ordered_delay[:, :, None] == jnp.arange(delay_table.shape[0])[None, None, :]
    delays = jnp.sum(jnp.where(picked, delay_table, 0.0), axis=-1)
    local_ids = sub_index * 2 + jnp.arange(2)
    local_freq = row_frequency(local_ids, subbands)
    angles = (2.0 * math.pi * delays)[None] * local_freq[:, None, None]
    scaling = 1.0 / math.sqrt(stations)
    w_real = (jnp.cos(angles) * scaling).astype(jnp.bfloat16)
    w_imag = (-jnp.sin(angles) * scaling).astype(jnp.bfloat16)
    live = (local_ids[:, None] >= ordered_bounds[None, :, 0]) & (
        local_ids[:, None] < ordered_bounds[None, :, 1]
    )
    blank = jnp.zeros((), jnp.bfloat16)
    w_real = jnp.where(live[:, :, None], w_real, blank)
    w_imag = jnp.where(live[:, :, None], w_imag, blank)
    weights = jnp.stack(
        [jnp.concatenate([w_real, -w_imag], axis=2), jnp.concatenate([w_imag, w_real], axis=2)], axis=2
    ).reshape(2, 2 * beams, 2 * stations)

    entry = lax.dynamic_index_in_dim(ordered_entry, my_x, axis=1, keepdims=False).reshape(CHUNKS * NY)
    bounds = lax.dynamic_index_in_dim(
        ordered_bounds.reshape(CHUNKS, NX, NY, 2), my_x, axis=1, keepdims=False
    ).reshape(CHUNKS * NY, 2)
    strength = jnp.sum(
        jnp.where(entry[:, None] == jnp.arange(dm_table.shape[0])[None, :], dm_table, 0.0), axis=-1
    )
    in_plane = lax.rem(sub_index, NZ * NY)
    parity = lax.rem(my_x + jnp.arange(2), 2)
    low_row = parity * (subbands // 4) + 2 * in_plane + core
    high_row = low_row + subbands // 2
    high_live = (high_row[None, :] >= bounds[:, :1]) & (high_row[None, :] < bounds[:, 1:])
    freq = row_frequency(jnp.where(high_live, high_row[None, :], low_row[None, :]), subbands)
    dispersion = (0.5 * strength[:, None] / (LENGTH * (freq * freq * freq))).reshape(-1)

    dfts, planes = dft_tables()
    cosine_poly, sine_poly = turn_coefficients()
    vmem = pl.BlockSpec(memory_space=pltpu.VMEM)
    gathered = pl.pallas_call(
        functools.partial(kernel, cosine_poly, sine_poly),
        out_shape=jax.ShapeDtypeStruct((2, NZ * NY * 2, SIDE, SIDE), jnp.bfloat16),
        in_specs=[vmem, vmem, vmem, vmem, pl.BlockSpec(memory_space=pltpu.SMEM)],
        out_specs=pl.BlockSpec(memory_space=pl.ANY),
        scratch_shapes=[
            pltpu.VMEM((2 * CHUNKS * NX, 16, QUARTER), jnp.bfloat16),
            pltpu.VMEM((CHUNKS, 2 * NX, 16, QUARTER), jnp.bfloat16),
            pltpu.VMEM((2, 2 * NY * SIDE, SIDE), jnp.float32),
            pltpu.VMEM((CHUNKS * NY * 2, 2, SIDE, SIDE), jnp.bfloat16),
            pltpu.SemaphoreType.DMA((CHUNKS,)),
            pltpu.SemaphoreType.DMA((CHUNKS,)),
            pltpu.SemaphoreType.DMA,
            pltpu.SemaphoreType.DMA,
            pltpu.SemaphoreType.DMA((CHUNKS + 1,)),
        ],
        compiler_params=pltpu.CompilerParams(
            collective_id=0, has_side_effects=True, vmem_limit_bytes=56 * 1024 * 1024
        ),
        name="beams",
    )(
        weights,
        voltages.reshape(2, 2 * stations, HALF),
        jnp.asarray(dfts),
        jnp.asarray(planes),
        dispersion,
    )

    rows = gathered.reshape(subbands // 2, SIDE // 2, 2, SIDE)
    rows = jnp.transpose(rows, (0, 2, 1, 3)).reshape(1, subbands // 2, 2, HALF)
    own_bounds = lax.dynamic_index_in_dim(range_bounds, own_beam, keepdims=False)
    ids = jnp.arange(subbands).reshape(2, subbands // 2, 1, 1)
    alive = (ids >= own_bounds[0]) & (ids < own_bounds[1])
    placed = jnp.where(alive, rows, jnp.zeros((), jnp.bfloat16))
    return placed.reshape(1, subbands, 2, HALF)


def solution(mesh):
    return jax.shard_map(
        per_device,
        mesh=mesh,
        in_specs=(P("sub", None, None, "section"), P(), P(), P(), P(), P()),
        out_specs=P("sub", None, None, "section"),
        check_vma=False,
    )
```

```python
import functools
import math

import jax
import jax.numpy as jnp
import numpy as np
from jax import lax
from jax.experimental import pallas as pl
from jax.experimental.pallas import tpu as pltpu
from jax.sharding import PartitionSpec as P

MESH = pl.DeviceIdType.MESH
NX, NZ, NY = 4, 8, 4
LENGTH = 16384
SIDE = 128
HALF = LENGTH // 2
PIECES = 4
PIECE = HALF // PIECES
PAIR = 2
CHUNKS = NZ * NY // PAIR
AHEAD = 3
LANES = 256


def chunk_offset(chunk):
    index = chunk // 2
    step = (index + 1) // 2
    return (NZ // 2 + step * (1 - 2 * (index % 2)) + NZ) % NZ


def split_table(table):
    high = table.astype(jnp.bfloat16)
    low = (table - high.astype(np.float64)).astype(jnp.bfloat16)
    return np.stack([high, low])


def dft_tables():
    index = np.arange(SIDE)
    angle = 2.0 * np.pi * (np.outer(index, index) % SIDE) / SIDE
    cosine, sine = np.cos(angle), np.sin(angle)
    first = np.block([[cosine, sine], [-sine, cosine]])
    first = first.reshape(2 * SIDE, 2, 2, 2, 2, PIECE // SIDE)
    first = first.transpose(0, 1, 4, 2, 3, 5).reshape(2 * SIDE, 2 * SIDE)
    second = np.block([[cosine, -sine], [sine, cosine]])
    third = np.block([[cosine, sine], [-sine, cosine]])
    fourth = np.empty((SIDE, 2, 2 * SIDE))
    fourth[:, 0] = np.concatenate([cosine, -sine], axis=1)
    fourth[:, 1] = np.concatenate([sine, cosine], axis=1)
    fourth = fourth.reshape(2 * SIDE, 2 * SIDE) / LENGTH
    dfts = np.stack([split_table(t) for t in (first, second, third, fourth)])
    twist = 2.0 * np.pi * np.outer(index, index) / LENGTH
    bins = index[:, None] + SIDE * np.where(index < SIDE // 2, index, index - SIDE)[None, :]
    planes = np.stack([np.cos(twist), np.sin(twist), (bins * bins).astype(np.float64)])
    return dfts, planes.astype(np.float32)


def turn_coefficients():
    grid = np.cos(np.pi * (np.arange(400) + 0.5) / 400) * 0.25 + 0.25
    x = np.sqrt(grid) * 0.5 / np.sqrt(0.5)
    square = x * x
    cosine = np.polynomial.chebyshev.Chebyshev.fit(square, np.cos(2 * np.pi * x), 6, domain=[0, 0.25])
    sine = np.polynomial.chebyshev.Chebyshev.fit(
        square, np.sin(2 * np.pi * x) / x, 6, domain=[0, 0.25]
    )
    power = np.polynomial.Polynomial
    return (
        [float(v) for v in cosine.convert(kind=power).coef],
        [float(v) for v in sine.convert(kind=power).coef],
    )


def horner(coefficients, x):
    total = coefficients[-1]
    for value in coefficients[-2::-1]:
        total = total * x + value
    return total


def split(value):
    high = value.astype(jnp.bfloat16)
    return high, (value - high.astype(jnp.float32)).astype(jnp.bfloat16)


def dot(left, right):
    return jnp.dot(left, right, preferred_element_type=jnp.float32)


def turn_cos_sin(turns, cosine_poly, sine_poly):
    turns = turns - jnp.round(turns)
    square = turns * turns
    return horner(cosine_poly, square), horner(sine_poly, square) * turns


def kernel(
    cosine_poly,
    sine_poly,
    delay_table,
    dm_table,
    dm_index,
    bounds_scalar,
    cubes,
    delay_index,
    bounds,
    voltages,
    dfts,
    planes,
    gathered,
    weights,
    formed,
    arrived,
    grid,
    results,
    x_send,
    x_recv,
    z_send,
    z_recv,
    own_sem,
):
    me = lax.axis_index("sub")
    core = lax.axis_index("section")
    my_x = me // (NZ * NY)
    my_z = lax.rem(me // NY, NZ)
    my_y = lax.rem(me, NY)
    plane_start = my_x * (NZ * NY)

    barrier = pltpu.get_barrier_semaphore()

    def x_partner(step):
        other_x = lax.rem(my_x - step // 2 + NX, NX)
        other_core = lax.rem(core + lax.rem(step, 2), 2)
        return other_x, other_core

    def greet_x(step, carry):
        other_x, other_core = x_partner(step)
        pl.semaphore_signal(
            barrier, inc=1, device_id=((other_x * NZ + my_z) * NY + my_y, other_core), device_id_type=MESH
        )
        return carry

    def greet_plane(step, carry):
        other = lax.rem(my_z * NY + my_y + step // 2, NZ * NY)
        other_core = lax.rem(core + lax.rem(step, 2), 2)
        pl.semaphore_signal(
            barrier, inc=1, device_id=(plane_start + other, other_core), device_id_type=MESH
        )
        return carry

    lax.fori_loop(2, 2 * NX, greet_x, 0)
    lax.fori_loop(1, 2 * NZ * NY, greet_plane, 0)

    beams = NX * NZ * NY
    stations = delay_index.shape[0]
    subbands = 2 * beams

    entries = delay_index[...]

    def look_up(entry, total):
        return jnp.where(entries == entry, delay_table[entry], total)

    delays = lax.fori_loop(
        0, delay_table.shape[0], look_up, jnp.zeros((stations, beams), jnp.float32), unroll=8
    )
    row = lax.broadcasted_iota(jnp.int32, (CHUNKS * NX * 8, 1), 0)
    row_chunk = row // (NX * 8)
    row_pair = (row // 2) % PAIR
    row_z = (my_z + (1 - 2 * row_pair) * chunk_offset(row_chunk) + NZ) % NZ
    row_beam = ((row // 8) % NX) * (NZ * NY) + row_z * NY + PAIR * row_pair + row_chunk % 2
    column = lax.broadcasted_iota(jnp.int32, (CHUNKS * NX * 8, 2 * beams), 1)
    chosen = jnp.where(column == (row % 2) * beams + row_beam, 1.0, 0.0).astype(jnp.bfloat16)
    piece_of_row = (row // 4) % 2
    piece_of_lane = lax.broadcasted_iota(jnp.int32, (CHUNKS * NX * 8, 4 * stations), 1) // (2 * stations)
    scaling = 1.0 / math.sqrt(stations)
    for local in range(2):
        subband = 2 * me + local
        freq = 1.0 + (subband.astype(jnp.float32) + 0.5) * (1.0 / subbands)
        cosine, sine = turn_cos_sin(delays * freq, cosine_poly, sine_poly)
        live = jnp.logical_and(bounds[0:1, :] <= subband, bounds[1:2, :] > subband)
        cosine = jnp.where(live, cosine * scaling, 0.0)
        sine = jnp.where(live, sine * scaling, 0.0)
        both = jnp.concatenate(
            [
                jnp.concatenate([cosine, -sine], axis=1),
                jnp.concatenate([sine, cosine], axis=1),
            ],
            axis=0,
        )
        source = jnp.concatenate([both, both], axis=0).astype(jnp.bfloat16)
        placed = lax.dot_general(
            chosen, source, (((1,), (1,)), ((), ())), preferred_element_type=jnp.float32
        )
        weights[local] = jnp.where(piece_of_row == piece_of_lane, placed, 0.0).astype(jnp.bfloat16)

    tiles = PIECE // LANES

    def form(step, carry):
        local = step // tiles
        start = lax.rem(step, tiles) * LANES
        parts = []
        for couple in range(2):
            blocks = [
                voltages[
                    local, :, pl.ds(pl.multiple_of((couple * 2 + piece) * PIECE + start, LANES), LANES)
                ]
                for piece in range(2)
            ]
            product = dot(weights[local], jnp.concatenate(blocks, axis=0))
            parts.append(product.reshape(CHUNKS * NX, 8, LANES))
        both = jnp.concatenate(parts, axis=1).astype(jnp.bfloat16)
        formed[
            pl.ds(local * (CHUNKS * NX), CHUNKS * NX), :, pl.ds(pl.multiple_of(start, LANES), LANES)
        ] = both
        return carry

    lax.fori_loop(0, 2 * tiles, form, 0)

    pl.semaphore_wait(barrier, 2 * NX - 2 + 2 * NZ * NY - 1)

    def x_copy(chunk, step):
        other_x, other_core = x_partner(step)
        return pltpu.make_async_remote_copy(
            src_ref=formed.at[(other_core * CHUNKS + chunk) * NX + other_x],
            dst_ref=arrived.at[chunk, step],
            send_sem=x_send.at[chunk],
            recv_sem=x_recv.at[chunk],
            device_id=((other_x * NZ + my_z) * NY + my_y, other_core),
            device_id_type=MESH,
        )

    def own_copy(chunk):
        return pltpu.make_async_copy(
            formed.at[(core * CHUNKS + chunk) * NX + my_x], arrived.at[chunk, 0], own_sem.at[chunk]
        )

    def start_x(chunk):
        def one(step, carry):
            x_copy(chunk, step).start()
            return carry

        lax.fori_loop(1, 2 * NX, one, 0)
        own_copy(chunk).start()

    def wait_x_sent(chunk):
        pltpu.make_async_copy(
            formed.at[pl.ds(0, 2 * NX - 1)], formed.at[pl.ds(0, 2 * NX - 1)], x_send.at[chunk]
        ).wait()

    for chunk in range(AHEAD):
        start_x(chunk)

    slot = (my_z * NY + my_y) * 2 + core

    def do_chunk(chunk, carry):
        pltpu.make_async_copy(
            arrived.at[chunk, pl.ds(1, 2 * NX - 1)],
            arrived.at[chunk, pl.ds(1, 2 * NX - 1)],
            x_recv.at[chunk],
        ).wait()
        own_copy(chunk).wait()

        @pl.when(chunk < CHUNKS - AHEAD)
        def _():
            start_x(chunk + AHEAD)

        offset = chunk_offset(chunk)

        def fold(step, carry):
            group = step // 2
            other = lax.rem(step, 2)
            half = lax.rem(core + other, 2)

            def lane_tile(index, carry):
                lanes = pl.ds(pl.multiple_of(index * SIDE, SIDE), SIDE)
                near = arrived[chunk, group * 2 + other, :, lanes].astype(jnp.float32)
                far = arrived[chunk, group * 2 + 4 + other, :, lanes].astype(jnp.float32)
                total = near + far
                row = half * (SIDE // 4) + index
                grid[group, pl.ds(row, 8, stride=SIDE // 2), :] = total[:8]
                grid[group, pl.ds(row + SIDE // 8, 8, stride=SIDE // 2), :] = total[8:]
                return carry

            lax.fori_loop(0, PIECE // SIDE, lane_tile, 0, unroll=4)
            return carry

        lax.fori_loop(0, 4, fold, 0)

        def transform(beam, carry):
            other_z = lax.rem(my_z + (1 - 2 * beam) * offset + NZ, NZ)
            other_y = PAIR * beam + lax.rem(chunk, 2)
            beam_id = plane_start + other_z * NY + other_y
            strength = dm_table[dm_index[beam_id]]
            series = []
            for group in range(2):
                pieces = [
                    grid[
                        group,
                        pl.ds(pl.multiple_of((piece * 4 + beam * 2) * (SIDE // 2) + part * (SIDE // 2), SIDE // 2), SIDE // 2),
                        :,
                    ]
                    for part in range(2)
                    for piece in range(2)
                ]
                series.append(jnp.concatenate(pieces, axis=0))
            series = jnp.concatenate(series, axis=1).astype(jnp.bfloat16)
            stage = dot(dfts[0, 0], series) + dot(dfts[0, 1], series)
            cosine, sine = planes[0], planes[1]
            turned = []
            for group in range(2):
                lanes = slice(group * SIDE, (group + 1) * SIDE)
                real, imag = stage[:SIDE, lanes], stage[SIDE:, lanes]
                turned.append(
                    jnp.concatenate([real * cosine + imag * sine, imag * cosine - real * sine], axis=1)
                )
            high, low = split(jnp.concatenate(turned, axis=0))
            stage = dot(high, dfts[1, 0]) + dot(high, dfts[1, 1]) + dot(low, dfts[1, 0])
            turned = []
            for group in range(2):
                rows_of = slice(group * SIDE, (group + 1) * SIDE)
                real, imag = stage[rows_of, :SIDE], stage[rows_of, SIDE:]
                low_row = lax.rem(my_x + group, 2) * (subbands // 4) + 2 * (my_z * NY + my_y) + core
                high_row = low_row + subbands // 2
                is_high = jnp.logical_and(
                    bounds_scalar[0, beam_id] <= high_row, bounds_scalar[1, beam_id] > high_row
                )
                dispersion = strength * cubes[jnp.where(is_high, high_row, low_row)]
                chirp_cos, chirp_sin = turn_cos_sin(dispersion * planes[2], cosine_poly, sine_poly)
                turned.append(
                    jnp.concatenate(
                        [real * chirp_cos - imag * chirp_sin, real * chirp_sin + imag * chirp_cos], axis=1
                    )
                )
            high, low = split(jnp.concatenate(turned, axis=0))
            stage = dot(high, dfts[2, 0]) + dot(high, dfts[2, 1]) + dot(low, dfts[2, 0])
            turned = []
            for group in range(2):
                rows_of = slice(group * SIDE, (group + 1) * SIDE)
                real, imag = stage[rows_of, :SIDE], stage[rows_of, SIDE:]
                turned.append(
                    jnp.concatenate([real * cosine - imag * sine, real * sine + imag * cosine], axis=0)
                )
            high, low = split(jnp.concatenate(turned, axis=1))
            final = dot(dfts[3, 0], high) + dot(dfts[3, 1], high) + dot(dfts[3, 0], low)
            final = final.astype(jnp.bfloat16)
            for section in range(2):
                message = (chunk * PAIR + beam) * 2 + section
                for group in range(2):
                    parity = lax.rem(my_x + group, 2)
                    results[message, parity] = final[
                        section * SIDE : (section + 1) * SIDE, group * SIDE : (group + 1) * SIDE
                    ]

            def send(section, carry):
                message = (chunk * PAIR + beam) * 2 + section
                own = jnp.logical_and(beam_id == me, section == core)

                @pl.when(own)
                def _():
                    pltpu.make_async_copy(
                        results.at[message], gathered.at[:, slot], own_sem.at[CHUNKS]
                    ).start()

                @pl.when(jnp.logical_not(own))
                def _():
                    pltpu.make_async_remote_copy(
                        src_ref=results.at[message],
                        dst_ref=gathered.at[:, slot],
                        send_sem=z_send,
                        recv_sem=z_recv,
                        device_id=(beam_id, section),
                        device_id_type=MESH,
                    ).start()

                return carry

            lax.fori_loop(0, 2, send, 0)
            return carry

        lax.fori_loop(0, PAIR, transform, 0)
        return carry

    lax.fori_loop(0, CHUNKS, do_chunk, 0)

    for chunk in range(CHUNKS):
        wait_x_sent(chunk)
    others = 2 * NZ * NY - 1
    pltpu.make_async_copy(
        results.at[0], gathered.at[:, slot], own_sem.at[CHUNKS]
    ).wait()
    pltpu.make_async_copy(results.at[pl.ds(0, others)], results.at[pl.ds(0, others)], z_send).wait()
    pltpu.make_async_copy(
        gathered.at[:, pl.ds(0, others)], gathered.at[:, pl.ds(0, others)], z_recv
    ).wait()


BLOCK = 16


def place_kernel(bounds, gathered, placed):
    me = lax.axis_index("sub")
    start, end = bounds[0, me], bounds[1, me]
    rows = placed.shape[1] * pl.num_programs(0)
    first = pl.program_id(0) * BLOCK
    for high in range(2):
        row = high * rows + first + lax.broadcasted_iota(jnp.int32, (BLOCK, 1, 1), 0)
        live = jnp.logical_and(row >= start, row < end)
        value = jnp.where(live, gathered[...].astype(jnp.float32), 0.0)
        placed[high] = value.astype(jnp.bfloat16)


def per_device(voltages, delay_table, delay_index, dm_table, dm_index, range_bounds):
    stations = voltages.shape[2]
    subbands = voltages.shape[0] * lax.axis_size("sub")
    frequency = 1.0 + (np.arange(subbands) + 0.5) / subbands
    cubes = (0.5 / (LENGTH * frequency**3)).astype(np.float32)
    dfts, planes = dft_tables()
    cosine_poly, sine_poly = turn_coefficients()
    vmem = pl.BlockSpec(memory_space=pltpu.VMEM)
    smem = pl.BlockSpec(memory_space=pltpu.SMEM)
    bounds = range_bounds.T
    gathered = pl.pallas_call(
        functools.partial(kernel, cosine_poly, sine_poly),
        out_shape=jax.ShapeDtypeStruct((2, NZ * NY * 2, SIDE, SIDE), jnp.bfloat16),
        in_specs=[smem] * 5 + [vmem] * 5,
        out_specs=pl.BlockSpec(memory_space=pl.ANY),
        scratch_shapes=[
            pltpu.VMEM((2, CHUNKS * NX * 8, 4 * stations), jnp.bfloat16),
            pltpu.VMEM((2 * CHUNKS * NX, 16, PIECE), jnp.bfloat16),
            pltpu.VMEM((CHUNKS, 2 * NX, 16, PIECE), jnp.bfloat16),
            pltpu.VMEM((2, 4 * SIDE, SIDE), jnp.float32),
            pltpu.VMEM((CHUNKS * PAIR * 2, 2, SIDE, SIDE), jnp.bfloat16),
            pltpu.SemaphoreType.DMA((CHUNKS,)),
            pltpu.SemaphoreType.DMA((CHUNKS,)),
            pltpu.SemaphoreType.DMA,
            pltpu.SemaphoreType.DMA,
            pltpu.SemaphoreType.DMA((CHUNKS + 1,)),
        ],
        compiler_params=pltpu.CompilerParams(
            collective_id=0, has_side_effects=True, vmem_limit_bytes=56 * 1024 * 1024
        ),
        name="beams",
    )(
        delay_table,
        dm_table,
        dm_index,
        bounds,
        jnp.asarray(cubes),
        delay_index.T,
        bounds,
        voltages.reshape(2, 2 * stations, HALF),
        jnp.asarray(dfts),
        jnp.asarray(planes),
    )

    rows = subbands // 2
    placed = pl.pallas_call(
        place_kernel,
        grid_spec=pltpu.PrefetchScalarGridSpec(
            num_scalar_prefetch=1,
            grid=(rows // BLOCK,),
            in_specs=[pl.BlockSpec((BLOCK, SIDE, SIDE), lambda i, bounds: (i, 0, 0))],
            out_specs=pl.BlockSpec((2, BLOCK, SIDE, SIDE), lambda i, bounds: (0, i, 0, 0)),
        ),
        out_shape=jax.ShapeDtypeStruct((2, rows, SIDE, SIDE), jnp.bfloat16),
        name="place",
    )(bounds, gathered.reshape(rows, SIDE, SIDE))
    placed = placed.reshape(subbands, SIDE // 2, 2, SIDE)
    return jnp.transpose(placed, (0, 2, 1, 3)).reshape(1, subbands, 2, HALF)


def solution(mesh):
    return jax.shard_map(
        per_device,
        mesh=mesh,
        in_specs=(P("sub", None, None, "section"), P(), P(), P(), P(), P()),
        out_specs=P("sub", None, None, "section"),
        check_vma=False,
    )
```

```python
import functools
import math

import jax
import jax.numpy as jnp
import numpy as np
from jax import lax
from jax.experimental import pallas as pl
from jax.experimental.pallas import tpu as pltpu
from jax.sharding import PartitionSpec as P

MESH = pl.DeviceIdType.MESH
NX, NZ, NY = 4, 8, 4
LENGTH = 16384
SIDE = 128
HALF = LENGTH // 2
PIECES = 4
PIECE = HALF // PIECES
PAIR = 2
CHUNKS = NZ * NY // PAIR
AHEAD = 2
LANES = 256


def chunk_offset(chunk):
    index = chunk // 2
    step = (index + 1) // 2
    return (NZ // 2 + step * (1 - 2 * (index % 2)) + NZ) % NZ


def split_table(table):
    high = table.astype(jnp.bfloat16)
    low = (table - high.astype(np.float64)).astype(jnp.bfloat16)
    return np.stack([high, low])


def dft_tables():
    index = np.arange(SIDE)
    angle = 2.0 * np.pi * (np.outer(index, index) % SIDE) / SIDE
    cosine, sine = np.cos(angle), np.sin(angle)
    first = np.block([[cosine, sine], [-sine, cosine]])
    first = first.reshape(2 * SIDE, 2, 2, 2, 2, PIECE // SIDE)
    first = first.transpose(0, 1, 4, 2, 3, 5).reshape(2 * SIDE, 2 * SIDE)
    second = np.block([[cosine, -sine], [sine, cosine]])
    third = np.block([[cosine, sine], [-sine, cosine]])
    fourth = np.empty((SIDE, 2, 2 * SIDE))
    fourth[:, 0] = np.concatenate([cosine, -sine], axis=1)
    fourth[:, 1] = np.concatenate([sine, cosine], axis=1)
    fourth = fourth.reshape(2 * SIDE, 2 * SIDE) / LENGTH
    dfts = np.stack([split_table(t) for t in (first, second, third, fourth)])
    twist = 2.0 * np.pi * np.outer(index, index) / LENGTH
    bins = index[:, None] + SIDE * np.where(index < SIDE // 2, index, index - SIDE)[None, :]
    planes = np.stack([np.cos(twist), np.sin(twist), (bins * bins).astype(np.float64)])
    return dfts, planes.astype(np.float32)


def turn_coefficients():
    grid = np.cos(np.pi * (np.arange(400) + 0.5) / 400) * 0.25 + 0.25
    x = np.sqrt(grid) * 0.5 / np.sqrt(0.5)
    square = x * x
    cosine = np.polynomial.chebyshev.Chebyshev.fit(square, np.cos(2 * np.pi * x), 6, domain=[0, 0.25])
    sine = np.polynomial.chebyshev.Chebyshev.fit(
        square, np.sin(2 * np.pi * x) / x, 6, domain=[0, 0.25]
    )
    power = np.polynomial.Polynomial
    return (
        [float(v) for v in cosine.convert(kind=power).coef],
        [float(v) for v in sine.convert(kind=power).coef],
    )


def horner(coefficients, x):
    total = coefficients[-1]
    for value in coefficients[-2::-1]:
        total = total * x + value
    return total


def split(value):
    high = value.astype(jnp.bfloat16)
    return high, (value - high.astype(jnp.float32)).astype(jnp.bfloat16)


def dot(left, right):
    return jnp.dot(left, right, preferred_element_type=jnp.float32)


def turn_cos_sin(turns, cosine_poly, sine_poly):
    turns = turns - jnp.round(turns)
    square = turns * turns
    return horner(cosine_poly, square), horner(sine_poly, square) * turns


def kernel(
    cosine_poly,
    sine_poly,
    delay_table,
    dm_table,
    dm_index,
    bounds_scalar,
    cubes,
    delay_index,
    bounds,
    voltages_far,
    dfts_far,
    planes_far,
    gathered,
    voltages,
    dfts,
    planes,
    weights,
    formed,
    arrived,
    grid,
    results,
    x_send,
    x_recv,
    z_send,
    z_recv,
    own_sem,
    load_sem,
):
    loads = [
        pltpu.make_async_copy(far, near, load_sem.at[index])
        for index, (far, near) in enumerate(
            [(voltages_far, voltages), (dfts_far, dfts), (planes_far, planes)]
        )
    ]
    for load in loads:
        load.start()

    me = lax.axis_index("sub")
    core = lax.axis_index("section")
    my_x = me // (NZ * NY)
    my_z = lax.rem(me // NY, NZ)
    my_y = lax.rem(me, NY)
    plane_start = my_x * (NZ * NY)

    barrier = pltpu.get_barrier_semaphore()

    def x_partner(step):
        other_x = lax.rem(my_x - step // 2 + NX, NX)
        other_core = lax.rem(core + lax.rem(step, 2), 2)
        return other_x, other_core

    def greet_x(step, carry):
        other_x, other_core = x_partner(step)
        pl.semaphore_signal(
            barrier, inc=1, device_id=((other_x * NZ + my_z) * NY + my_y, other_core), device_id_type=MESH
        )
        return carry

    def greet_plane(step, carry):
        other = lax.rem(my_z * NY + my_y + step // 2, NZ * NY)
        other_core = lax.rem(core + lax.rem(step, 2), 2)
        pl.semaphore_signal(
            barrier, inc=1, device_id=(plane_start + other, other_core), device_id_type=MESH
        )
        return carry

    lax.fori_loop(2, 2 * NX, greet_x, 0)
    lax.fori_loop(1, 2 * NZ * NY, greet_plane, 0)

    beams = NX * NZ * NY
    stations = delay_index.shape[0]
    subbands = 2 * beams

    entries = delay_index[...]

    def look_up(entry, total):
        return jnp.where(entries == entry, delay_table[entry], total)

    delays = lax.fori_loop(
        0, delay_table.shape[0], look_up, jnp.zeros((stations, beams), jnp.float32), unroll=8
    )
    row = lax.broadcasted_iota(jnp.int32, (CHUNKS * NX * 8, 1), 0)
    row_chunk = row >> 5
    row_index = row_chunk >> 1
    row_offset = NZ // 2 + ((row_index + 1) >> 1) * (1 - 2 * (row_index & 1))
    row_pair = (row >> 1) & 1
    row_z = (my_z + (1 - 2 * row_pair) * row_offset + 2 * NZ) & (NZ - 1)
    row_beam = ((row >> 3) & (NX - 1)) * (NZ * NY) + row_z * NY + PAIR * row_pair + (row_chunk & 1)
    column = lax.broadcasted_iota(jnp.int32, (CHUNKS * NX * 8, 2 * beams), 1)
    chosen = jnp.where(column == (row & 1) * beams + row_beam, 1.0, 0.0).astype(jnp.bfloat16)
    piece_of_row = (row >> 2) & 1
    lane = lax.broadcasted_iota(jnp.int32, (CHUNKS * NX * 8, 4 * stations), 1)
    piece_of_lane = jnp.where(lane >= 2 * stations, 1, 0)
    scaling = 1.0 / math.sqrt(stations)
    for local in range(2):
        subband = 2 * me + local
        freq = 1.0 + (subband.astype(jnp.float32) + 0.5) * (1.0 / subbands)
        cosine, sine = turn_cos_sin(delays * freq, cosine_poly, sine_poly)
        live = jnp.logical_and(bounds[0:1, :] <= subband, bounds[1:2, :] > subband)
        cosine = jnp.where(live, cosine * scaling, 0.0)
        sine = jnp.where(live, sine * scaling, 0.0)
        both = jnp.concatenate(
            [
                jnp.concatenate([cosine, -sine], axis=1),
                jnp.concatenate([sine, cosine], axis=1),
            ],
            axis=0,
        )
        source = jnp.concatenate([both, both], axis=0).astype(jnp.bfloat16)
        placed = lax.dot_general(
            chosen, source, (((1,), (1,)), ((), ())), preferred_element_type=jnp.float32
        )
        weights[local] = jnp.where(piece_of_row == piece_of_lane, placed, 0.0).astype(jnp.bfloat16)

    tiles = PIECE // LANES

    def form(first, count, step, carry):
        local = step // tiles
        start = lax.rem(step, tiles) * LANES
        parts = []
        for couple in range(2):
            blocks = [
                voltages[
                    local, :, pl.ds(pl.multiple_of((couple * 2 + piece) * PIECE + start, LANES), LANES)
                ]
                for piece in range(2)
            ]
            product = dot(
                weights[local, first * NX * 8 : (first + count) * NX * 8],
                jnp.concatenate(blocks, axis=0),
            )
            parts.append(product.reshape(count * NX, 8, LANES))
        both = jnp.concatenate(parts, axis=1).astype(jnp.bfloat16)
        formed[
            pl.ds(local * (CHUNKS * NX) + first * NX, count * NX),
            :,
            pl.ds(pl.multiple_of(start, LANES), LANES),
        ] = both
        return carry

    loads[0].wait()
    lax.fori_loop(0, 2 * tiles, functools.partial(form, 0, 1), 0)

    pl.semaphore_wait(barrier, 2 * NX - 2 + 2 * NZ * NY - 1)

    def x_copy(chunk, step):
        other_x, other_core = x_partner(step)
        return pltpu.make_async_remote_copy(
            src_ref=formed.at[(other_core * CHUNKS + chunk) * NX + other_x],
            dst_ref=arrived.at[chunk, step],
            send_sem=x_send.at[chunk],
            recv_sem=x_recv.at[chunk],
            device_id=((other_x * NZ + my_z) * NY + my_y, other_core),
            device_id_type=MESH,
        )

    def own_copy(chunk):
        return pltpu.make_async_copy(
            formed.at[(core * CHUNKS + chunk) * NX + my_x], arrived.at[chunk, 0], own_sem.at[chunk]
        )

    def start_x(chunk):
        def one(step, carry):
            x_copy(chunk, step).start()
            return carry

        lax.fori_loop(1, 2 * NX, one, 0)
        own_copy(chunk).start()

    def wait_x_sent(chunk):
        pltpu.make_async_copy(
            formed.at[pl.ds(0, 2 * NX - 1)], formed.at[pl.ds(0, 2 * NX - 1)], x_send.at[chunk]
        ).wait()

    start_x(0)
    lax.fori_loop(0, 2 * tiles, functools.partial(form, 1, CHUNKS - 1), 0)
    for load in loads[1:]:
        load.wait()
    wait_x_sent(0)
    start_x(1)

    slot = (my_z * NY + my_y) * 2 + core

    def do_chunk(chunk, carry):
        pltpu.make_async_copy(
            arrived.at[chunk, pl.ds(1, 2 * NX - 1)],
            arrived.at[chunk, pl.ds(1, 2 * NX - 1)],
            x_recv.at[chunk],
        ).wait()
        own_copy(chunk).wait()

        @pl.when(chunk < CHUNKS - AHEAD)
        def _():
            start_x(chunk + AHEAD)

        offset = chunk_offset(chunk)

        def fold(step, carry):
            group = step // 2
            other = lax.rem(step, 2)
            half = lax.rem(core + other, 2)

            def lane_tile(index, carry):
                lanes = pl.ds(pl.multiple_of(index * SIDE, SIDE), SIDE)
                near = arrived[chunk, group * 2 + other, :, lanes].astype(jnp.float32)
                far = arrived[chunk, group * 2 + 4 + other, :, lanes].astype(jnp.float32)
                total = near + far
                row = half * (SIDE // 4) + index
                grid[group, pl.ds(row, 8, stride=SIDE // 2), :] = total[:8]
                grid[group, pl.ds(row + SIDE // 8, 8, stride=SIDE // 2), :] = total[8:]
                return carry

            lax.fori_loop(0, PIECE // SIDE, lane_tile, 0, unroll=4)
            return carry

        lax.fori_loop(0, 4, fold, 0)

        def transform(beam, carry):
            other_z = lax.rem(my_z + (1 - 2 * beam) * offset + NZ, NZ)
            other_y = PAIR * beam + lax.rem(chunk, 2)
            beam_id = plane_start + other_z * NY + other_y
            strength = dm_table[dm_index[beam_id]]
            series = []
            for group in range(2):
                pieces = [
                    grid[
                        group,
                        pl.ds(pl.multiple_of((piece * 4 + beam * 2) * (SIDE // 2) + part * (SIDE // 2), SIDE // 2), SIDE // 2),
                        :,
                    ]
                    for part in range(2)
                    for piece in range(2)
                ]
                series.append(jnp.concatenate(pieces, axis=0))
            series = jnp.concatenate(series, axis=1).astype(jnp.bfloat16)
            stage = dot(dfts[0, 0], series) + dot(dfts[0, 1], series)
            cosine, sine = planes[0], planes[1]
            turned = []
            for group in range(2):
                lanes = slice(group * SIDE, (group + 1) * SIDE)
                real, imag = stage[:SIDE, lanes], stage[SIDE:, lanes]
                turned.append(
                    jnp.concatenate([real * cosine + imag * sine, imag * cosine - real * sine], axis=1)
                )
            high, low = split(jnp.concatenate(turned, axis=0))
            stage = dot(high, dfts[1, 0]) + dot(high, dfts[1, 1]) + dot(low, dfts[1, 0])
            turned = []
            for group in range(2):
                rows_of = slice(group * SIDE, (group + 1) * SIDE)
                real, imag = stage[rows_of, :SIDE], stage[rows_of, SIDE:]
                low_row = lax.rem(my_x + group, 2) * (subbands // 4) + 2 * (my_z * NY + my_y) + core
                high_row = low_row + subbands // 2
                is_high = jnp.logical_and(
                    bounds_scalar[0, beam_id] <= high_row, bounds_scalar[1, beam_id] > high_row
                )
                dispersion = strength * cubes[jnp.where(is_high, high_row, low_row)]
                chirp_cos, chirp_sin = turn_cos_sin(dispersion * planes[2], cosine_poly, sine_poly)
                turned.append(
                    jnp.concatenate(
                        [real * chirp_cos - imag * chirp_sin, real * chirp_sin + imag * chirp_cos], axis=1
                    )
                )
            high, low = split(jnp.concatenate(turned, axis=0))
            stage = dot(high, dfts[2, 0]) + dot(high, dfts[2, 1]) + dot(low, dfts[2, 0])
            turned = []
            for group in range(2):
                rows_of = slice(group * SIDE, (group + 1) * SIDE)
                real, imag = stage[rows_of, :SIDE], stage[rows_of, SIDE:]
                turned.append(
                    jnp.concatenate([real * cosine - imag * sine, real * sine + imag * cosine], axis=0)
                )
            high, low = split(jnp.concatenate(turned, axis=1))
            final = dot(dfts[3, 0], high) + dot(dfts[3, 1], high) + dot(dfts[3, 0], low)
            final = final.astype(jnp.bfloat16)
            for section in range(2):
                message = (chunk * PAIR + beam) * 2 + section
                for group in range(2):
                    parity = lax.rem(my_x + group, 2)
                    results[message, parity] = final[
                        section * SIDE : (section + 1) * SIDE, group * SIDE : (group + 1) * SIDE
                    ]

            def send(section, carry):
                message = (chunk * PAIR + beam) * 2 + section
                own = jnp.logical_and(beam_id == me, section == core)

                @pl.when(own)
                def _():
                    pltpu.make_async_copy(
                        results.at[message], gathered.at[:, slot], own_sem.at[CHUNKS]
                    ).start()

                @pl.when(jnp.logical_not(own))
                def _():
                    pltpu.make_async_remote_copy(
                        src_ref=results.at[message],
                        dst_ref=gathered.at[:, slot],
                        send_sem=z_send,
                        recv_sem=z_recv,
                        device_id=(beam_id, section),
                        device_id_type=MESH,
                    ).start()

                return carry

            lax.fori_loop(0, 2, send, 0)
            return carry

        lax.fori_loop(0, PAIR, transform, 0)
        return carry

    lax.fori_loop(0, CHUNKS, do_chunk, 0)

    for chunk in range(1, CHUNKS):
        wait_x_sent(chunk)
    others = 2 * NZ * NY - 1
    pltpu.make_async_copy(
        results.at[0], gathered.at[:, slot], own_sem.at[CHUNKS]
    ).wait()
    pltpu.make_async_copy(results.at[pl.ds(0, others)], results.at[pl.ds(0, others)], z_send).wait()
    pltpu.make_async_copy(
        gathered.at[:, pl.ds(0, others)], gathered.at[:, pl.ds(0, others)], z_recv
    ).wait()


BLOCK = 8
PARTS = 4


def place_kernel(bounds, gathered, placed, rows, blank, in_sem, out_sem):
    me = lax.axis_index("sub")
    start, end = bounds[0, me], bounds[1, me]
    count = gathered.shape[0]
    part = count // PARTS
    loads = [
        pltpu.make_async_copy(
            gathered.at[pl.ds(p * part, part)], rows.at[pl.ds(p * part, part)], in_sem.at[p]
        )
        for p in range(PARTS)
    ]
    for load in loads:
        load.start()
    blank[...] = jnp.zeros_like(blank)

    def write_blank(block, carry):
        first = block * BLOCK

        @pl.when(jnp.logical_or(first + BLOCK <= start, first >= end))
        def _():
            pltpu.make_async_copy(blank, placed.at[pl.ds(first, BLOCK)], out_sem).start()

        return carry

    lax.fori_loop(0, 2 * count // BLOCK, write_blank, 0)

    def write_rows(block, carry):
        source = block * BLOCK
        for high in range(2):
            first = source + high * count
            whole = jnp.logical_and(first >= start, first + BLOCK <= end)
            some = jnp.logical_and(first < end, first + BLOCK > start)

            @pl.when(whole)
            def _():
                pltpu.make_async_copy(
                    rows.at[pl.ds(source, BLOCK)], placed.at[pl.ds(first, BLOCK)], out_sem
                ).start()

            @pl.when(jnp.logical_and(some, jnp.logical_not(whole)))
            def _():
                def one(index, carry):
                    row = first + index
                    live = jnp.logical_and(row >= start, row < end)

                    @pl.when(live)
                    def _():
                        pltpu.make_async_copy(
                            rows.at[pl.ds(source + index, 1)], placed.at[pl.ds(row, 1)], out_sem
                        ).start()

                    @pl.when(jnp.logical_not(live))
                    def _():
                        pltpu.make_async_copy(
                            blank.at[pl.ds(0, 1)], placed.at[pl.ds(row, 1)], out_sem
                        ).start()

                    return carry

                lax.fori_loop(0, BLOCK, one, 0)

        return carry

    blocks = part // BLOCK
    for p in range(PARTS):
        loads[p].wait()
        lax.fori_loop(p * blocks, (p + 1) * blocks, write_rows, 0)
    pltpu.make_async_copy(placed, placed, out_sem).wait()


def per_device(voltages, delay_table, delay_index, dm_table, dm_index, range_bounds):
    stations = voltages.shape[2]
    subbands = voltages.shape[0] * lax.axis_size("sub")
    frequency = 1.0 + (np.arange(subbands) + 0.5) / subbands
    cubes = (0.5 / (LENGTH * frequency**3)).astype(np.float32)
    dfts, planes = dft_tables()
    cosine_poly, sine_poly = turn_coefficients()
    vmem = pl.BlockSpec(memory_space=pltpu.VMEM)
    smem = pl.BlockSpec(memory_space=pltpu.SMEM)
    far = pl.BlockSpec(memory_space=pl.ANY)
    bounds = range_bounds.T
    gathered = pl.pallas_call(
        functools.partial(kernel, cosine_poly, sine_poly),
        out_shape=jax.ShapeDtypeStruct((2, NZ * NY * 2, SIDE, SIDE), jnp.bfloat16),
        in_specs=[smem] * 5 + [vmem] * 2 + [far] * 3,
        out_specs=far,
        scratch_shapes=[
            pltpu.VMEM((2, 2 * stations, HALF), jnp.bfloat16),
            pltpu.VMEM(dfts.shape, dfts.dtype),
            pltpu.VMEM(planes.shape, planes.dtype),
            pltpu.VMEM((2, CHUNKS * NX * 8, 4 * stations), jnp.bfloat16),
            pltpu.VMEM((2 * CHUNKS * NX, 16, PIECE), jnp.bfloat16),
            pltpu.VMEM((CHUNKS, 2 * NX, 16, PIECE), jnp.bfloat16),
            pltpu.VMEM((2, 4 * SIDE, SIDE), jnp.float32),
            pltpu.VMEM((CHUNKS * PAIR * 2, 2, SIDE, SIDE), jnp.bfloat16),
            pltpu.SemaphoreType.DMA((CHUNKS,)),
            pltpu.SemaphoreType.DMA((CHUNKS,)),
            pltpu.SemaphoreType.DMA,
            pltpu.SemaphoreType.DMA,
            pltpu.SemaphoreType.DMA((CHUNKS + 1,)),
            pltpu.SemaphoreType.DMA((3,)),
        ],
        compiler_params=pltpu.CompilerParams(
            collective_id=0, has_side_effects=True, vmem_limit_bytes=56 * 1024 * 1024
        ),
        name="beams",
    )(
        delay_table,
        dm_table,
        dm_index,
        bounds,
        jnp.asarray(cubes),
        delay_index.T,
        bounds,
        voltages.reshape(2, 2 * stations, HALF),
        jnp.asarray(dfts),
        jnp.asarray(planes),
    )

    rows = subbands // 2
    placed = pl.pallas_call(
        place_kernel,
        in_specs=[smem, far],
        out_specs=far,
        out_shape=jax.ShapeDtypeStruct((subbands, SIDE, SIDE), jnp.bfloat16),
        scratch_shapes=[
            pltpu.VMEM((rows, SIDE, SIDE), jnp.bfloat16),
            pltpu.VMEM((BLOCK, SIDE, SIDE), jnp.bfloat16),
            pltpu.SemaphoreType.DMA((PARTS,)),
            pltpu.SemaphoreType.DMA,
        ],
        compiler_params=pltpu.CompilerParams(vmem_limit_bytes=56 * 1024 * 1024),
        name="place",
    )(bounds, gathered.reshape(rows, SIDE, SIDE))
    placed = placed.reshape(subbands, SIDE // 2, 2, SIDE)
    return jnp.transpose(placed, (0, 2, 1, 3)).reshape(1, subbands, 2, HALF)


def solution(mesh):
    return jax.shard_map(
        per_device,
        mesh=mesh,
        in_specs=(P("sub", None, None, "section"), P(), P(), P(), P(), P()),
        out_specs=P("sub", None, None, "section"),
        check_vma=False,
    )
```

```python
import functools
import math

import jax
import jax.numpy as jnp
import numpy as np
from jax import lax
from jax.experimental import pallas as pl
from jax.experimental.pallas import tpu as pltpu
from jax.sharding import PartitionSpec as P

MESH = pl.DeviceIdType.MESH
NX, NZ, NY = 4, 8, 4
LENGTH = 16384
SIDE = 128
HALF = LENGTH // 2
PIECES = 4
PIECE = HALF // PIECES
PAIR = 2
CHUNKS = NZ * NY // PAIR
AHEAD = 2
LANES = 256


def chunk_offset(chunk):
    index = chunk // 2
    step = (index + 1) // 2
    return (NZ // 2 + step * (1 - 2 * (index % 2)) + NZ) % NZ


def split_table(table):
    high = table.astype(jnp.bfloat16)
    low = (table - high.astype(np.float64)).astype(jnp.bfloat16)
    return np.stack([high, low])


def dft_tables():
    index = np.arange(SIDE)
    angle = 2.0 * np.pi * (np.outer(index, index) % SIDE) / SIDE
    cosine, sine = np.cos(angle), np.sin(angle)
    first = np.block([[cosine, sine], [-sine, cosine]])
    first = first.reshape(2 * SIDE, 2, 2, 2, 2, PIECE // SIDE)
    first = first.transpose(0, 1, 4, 2, 3, 5).reshape(2 * SIDE, 2 * SIDE)
    second = np.block([[cosine, -sine], [sine, cosine]])
    third = np.block([[cosine, sine], [-sine, cosine]])
    fourth = np.empty((SIDE, 2, 2 * SIDE))
    fourth[:, 0] = np.concatenate([cosine, -sine], axis=1)
    fourth[:, 1] = np.concatenate([sine, cosine], axis=1)
    fourth = fourth.reshape(2 * SIDE, 2 * SIDE) / LENGTH
    dfts = np.stack([split_table(t) for t in (first, second, third, fourth)])
    twist = 2.0 * np.pi * np.outer(index, index) / LENGTH
    bins = index[:, None] + SIDE * np.where(index < SIDE // 2, index, index - SIDE)[None, :]
    planes = np.stack([np.cos(twist), np.sin(twist), (bins * bins).astype(np.float64)])
    return dfts, planes.astype(np.float32)


def turn_coefficients():
    grid = np.cos(np.pi * (np.arange(400) + 0.5) / 400) * 0.25 + 0.25
    x = np.sqrt(grid) * 0.5 / np.sqrt(0.5)
    square = x * x
    cosine = np.polynomial.chebyshev.Chebyshev.fit(square, np.cos(2 * np.pi * x), 6, domain=[0, 0.25])
    sine = np.polynomial.chebyshev.Chebyshev.fit(
        square, np.sin(2 * np.pi * x) / x, 6, domain=[0, 0.25]
    )
    power = np.polynomial.Polynomial
    return (
        [float(v) for v in cosine.convert(kind=power).coef],
        [float(v) for v in sine.convert(kind=power).coef],
    )


def horner(coefficients, x):
    total = coefficients[-1]
    for value in coefficients[-2::-1]:
        total = total * x + value
    return total


def split(value):
    high = value.astype(jnp.bfloat16)
    return high, (value - high.astype(jnp.float32)).astype(jnp.bfloat16)


def dot(left, right):
    return jnp.dot(left, right, preferred_element_type=jnp.float32)


def turn_cos_sin(turns, cosine_poly, sine_poly):
    turns = turns - jnp.round(turns)
    square = turns * turns
    return horner(cosine_poly, square), horner(sine_poly, square) * turns


def kernel(
    cosine_poly,
    sine_poly,
    delay_table,
    dm_table,
    dm_index,
    bounds_scalar,
    cubes,
    delay_index,
    bounds,
    voltages_far,
    dfts_far,
    planes_far,
    gathered,
    voltages,
    dfts,
    planes,
    weights,
    formed,
    arrived,
    grid,
    results,
    x_send,
    x_recv,
    z_send,
    z_recv,
    own_sem,
    load_sem,
):
    loads = [
        pltpu.make_async_copy(far, near, load_sem.at[index])
        for index, (far, near) in enumerate(
            [(voltages_far, voltages), (dfts_far, dfts), (planes_far, planes)]
        )
    ]
    for load in loads:
        load.start()

    me = lax.axis_index("sub")
    core = lax.axis_index("section")
    my_x = me // (NZ * NY)
    my_z = lax.rem(me // NY, NZ)
    my_y = lax.rem(me, NY)
    plane_start = my_x * (NZ * NY)

    barrier = pltpu.get_barrier_semaphore()

    def x_partner(step):
        other_x = lax.rem(my_x - step // 2 + NX, NX)
        other_core = lax.rem(core + lax.rem(step, 2), 2)
        return other_x, other_core

    def greet_x(step, carry):
        other_x, other_core = x_partner(step)
        pl.semaphore_signal(
            barrier, inc=1, device_id=((other_x * NZ + my_z) * NY + my_y, other_core), device_id_type=MESH
        )
        return carry

    def greet_plane(step, carry):
        other = lax.rem(my_z * NY + my_y + step // 2, NZ * NY)
        other_core = lax.rem(core + lax.rem(step, 2), 2)
        pl.semaphore_signal(
            barrier, inc=1, device_id=(plane_start + other, other_core), device_id_type=MESH
        )
        return carry

    lax.fori_loop(2, 2 * NX, greet_x, 0)
    lax.fori_loop(1, 2 * NZ * NY, greet_plane, 0)

    beams = NX * NZ * NY
    stations = delay_index.shape[0]
    subbands = 2 * beams

    entries = delay_index[...]

    def look_up(entry, total):
        return jnp.where(entries == entry, delay_table[entry], total)

    delays = lax.fori_loop(
        0, delay_table.shape[0], look_up, jnp.zeros((stations, beams), jnp.float32), unroll=8
    )
    scaling = 1.0 / math.sqrt(stations)
    sources = []
    for local in range(2):
        subband = 2 * me + local
        freq = 1.0 + (subband.astype(jnp.float32) + 0.5) * (1.0 / subbands)
        cosine, sine = turn_cos_sin(delays * freq, cosine_poly, sine_poly)
        live = jnp.logical_and(bounds[0:1, :] <= subband, bounds[1:2, :] > subband)
        cosine = jnp.where(live, cosine * scaling, 0.0)
        sine = jnp.where(live, sine * scaling, 0.0)
        both = jnp.concatenate(
            [
                jnp.concatenate([cosine, -sine], axis=1),
                jnp.concatenate([sine, cosine], axis=1),
            ],
            axis=0,
        )
        sources.append(jnp.concatenate([both, both], axis=0).astype(jnp.bfloat16))

    def weigh(first, count):
        height = count * NX * 8
        row = first * NX * 8 + lax.broadcasted_iota(jnp.int32, (height, 1), 0)
        row_chunk = row >> 5
        row_index = row_chunk >> 1
        row_offset = NZ // 2 + ((row_index + 1) >> 1) * (1 - 2 * (row_index & 1))
        row_pair = (row >> 1) & 1
        row_z = (my_z + (1 - 2 * row_pair) * row_offset + 2 * NZ) & (NZ - 1)
        row_y = (my_y + PAIR * row_pair + (row_chunk & 1)) & (NY - 1)
        row_beam = ((row >> 3) & (NX - 1)) * (NZ * NY) + row_z * NY + row_y
        column = lax.broadcasted_iota(jnp.int32, (height, 2 * beams), 1)
        chosen = jnp.where(column == (row & 1) * beams + row_beam, 1.0, 0.0).astype(jnp.bfloat16)
        lane = lax.broadcasted_iota(jnp.int32, (height, 4 * stations), 1)
        same = ((row >> 2) & 1) == jnp.where(lane >= 2 * stations, 1, 0)
        for local in range(2):
            placed = lax.dot_general(
                chosen, sources[local], (((1,), (1,)), ((), ())), preferred_element_type=jnp.float32
            )
            weights[local, first * NX * 8 : (first + count) * NX * 8] = jnp.where(
                same, placed, 0.0
            ).astype(jnp.bfloat16)

    weigh(0, 1)
    tiles = PIECE // LANES

    def form(first, count, step, carry):
        local = step // tiles
        start = lax.rem(step, tiles) * LANES
        parts = []
        for couple in range(2):
            blocks = [
                voltages[
                    local, :, pl.ds(pl.multiple_of((couple * 2 + piece) * PIECE + start, LANES), LANES)
                ]
                for piece in range(2)
            ]
            product = dot(
                weights[local, first * NX * 8 : (first + count) * NX * 8],
                jnp.concatenate(blocks, axis=0),
            )
            parts.append(product.reshape(count * NX, 8, LANES))
        both = jnp.concatenate(parts, axis=1).astype(jnp.bfloat16)
        formed[
            pl.ds(local * (CHUNKS * NX) + first * NX, count * NX),
            :,
            pl.ds(pl.multiple_of(start, LANES), LANES),
        ] = both
        return carry

    loads[0].wait()
    lax.fori_loop(0, 2 * tiles, functools.partial(form, 0, 1), 0)

    pl.semaphore_wait(barrier, 2 * NX - 2 + 2 * NZ * NY - 1)

    def x_copy(chunk, step):
        other_x, other_core = x_partner(step)
        group = lax.rem(step // 2, 2)
        place = group * NX + (step // NX) * 2 + lax.rem(step, 2)
        return pltpu.make_async_remote_copy(
            src_ref=formed.at[(other_core * CHUNKS + chunk) * NX + other_x],
            dst_ref=arrived.at[chunk, place],
            send_sem=x_send.at[chunk],
            recv_sem=x_recv.at[chunk * 2 + group],
            device_id=((other_x * NZ + my_z) * NY + my_y, other_core),
            device_id_type=MESH,
        )

    def own_copy(chunk):
        return pltpu.make_async_copy(
            formed.at[(core * CHUNKS + chunk) * NX + my_x], arrived.at[chunk, 0], own_sem.at[chunk]
        )

    def start_x(chunk):
        def one(step, carry):
            x_copy(chunk, step).start()
            return carry

        lax.fori_loop(NX, NX + 2, one, 0)
        x_copy(chunk, 1).start()
        own_copy(chunk).start()
        lax.fori_loop(2, NX, one, 0)
        lax.fori_loop(NX + 2, 2 * NX, one, 0)

    def wait_x_sent(chunk):
        pltpu.make_async_copy(
            formed.at[pl.ds(0, 2 * NX - 1)], formed.at[pl.ds(0, 2 * NX - 1)], x_send.at[chunk]
        ).wait()

    start_x(0)
    weigh(1, CHUNKS - 1)
    lax.fori_loop(0, 2 * tiles, functools.partial(form, 1, CHUNKS - 1), 0)
    for load in loads[1:]:
        load.wait()
    wait_x_sent(0)
    start_x(1)

    slot = (my_z * NY + my_y) * 2 + core

    def do_half(step, carry):
        chunk = step // 2
        group = lax.rem(step, 2)

        @pl.when(group == 0)
        def _():
            near = arrived.at[chunk, pl.ds(1, NX - 1)]
            pltpu.make_async_copy(near, near, x_recv.at[step]).wait()
            own_copy(chunk).wait()

            @pl.when(chunk < CHUNKS - AHEAD)
            def _():
                start_x(chunk + AHEAD)

        @pl.when(group == 1)
        def _():
            far = arrived.at[chunk, pl.ds(NX, NX)]
            pltpu.make_async_copy(far, far, x_recv.at[step]).wait()

        offset = chunk_offset(chunk)
        parity = lax.rem(my_x + group, 2)

        def fold(other, carry):
            half = lax.rem(core + other, 2)

            def lane_tile(index, carry):
                lanes = pl.ds(pl.multiple_of(index * SIDE, SIDE), SIDE)
                near = arrived[chunk, group * NX + other, :, lanes].astype(jnp.float32)
                far = arrived[chunk, group * NX + 2 + other, :, lanes].astype(jnp.float32)
                total = near + far
                row = half * (SIDE // 4) + index
                grid[pl.ds(row, 8, stride=SIDE // 2), :] = total[:8]
                grid[pl.ds(row + SIDE // 8, 8, stride=SIDE // 2), :] = total[8:]
                return carry

            lax.fori_loop(0, PIECE // SIDE, lane_tile, 0, unroll=4)
            return carry

        lax.fori_loop(0, 2, fold, 0)

        def target_beam(beam):
            other_z = lax.rem(my_z + (1 - 2 * beam) * offset + NZ, NZ)
            other_y = lax.rem(my_y + PAIR * beam + lax.rem(chunk, 2), NY)
            return plane_start + other_z * NY + other_y

        series = []
        for beam in range(PAIR):
            pieces = [
                grid[pl.ds((piece * 4 + beam * 2 + part) * (SIDE // 2), SIDE // 2), :]
                for part in range(2)
                for piece in range(2)
            ]
            series.append(jnp.concatenate(pieces, axis=0))
        series = jnp.concatenate(series, axis=1).astype(jnp.bfloat16)
        low_row = parity * (subbands // 4) + 2 * (my_z * NY + my_y) + core
        high_row = low_row + subbands // 2
        stage = dot(dfts[0, 0], series) + dot(dfts[0, 1], series)
        cosine, sine = planes[0], planes[1]
        turned = []
        for beam in range(PAIR):
            lanes = slice(beam * SIDE, (beam + 1) * SIDE)
            real, imag = stage[:SIDE, lanes], stage[SIDE:, lanes]
            turned.append(
                jnp.concatenate([real * cosine + imag * sine, imag * cosine - real * sine], axis=1)
            )
        high, low = split(jnp.concatenate(turned, axis=0))
        stage = dot(high, dfts[1, 0]) + dot(high, dfts[1, 1]) + dot(low, dfts[1, 0])
        turned = []
        for beam in range(PAIR):
            rows_of = slice(beam * SIDE, (beam + 1) * SIDE)
            real, imag = stage[rows_of, :SIDE], stage[rows_of, SIDE:]
            beam_id = target_beam(beam)
            is_high = jnp.logical_and(
                bounds_scalar[0, beam_id] <= high_row, bounds_scalar[1, beam_id] > high_row
            )
            strength = dm_table[dm_index[beam_id]]
            dispersion = strength * cubes[jnp.where(is_high, high_row, low_row)]
            chirp_cos, chirp_sin = turn_cos_sin(dispersion * planes[2], cosine_poly, sine_poly)
            turned.append(
                jnp.concatenate(
                    [real * chirp_cos - imag * chirp_sin, real * chirp_sin + imag * chirp_cos], axis=1
                )
            )
        high, low = split(jnp.concatenate(turned, axis=0))
        stage = dot(high, dfts[2, 0]) + dot(high, dfts[2, 1]) + dot(low, dfts[2, 0])
        turned = []
        for beam in range(PAIR):
            rows_of = slice(beam * SIDE, (beam + 1) * SIDE)
            real, imag = stage[rows_of, :SIDE], stage[rows_of, SIDE:]
            turned.append(
                jnp.concatenate([real * cosine - imag * sine, real * sine + imag * cosine], axis=0)
            )
        high, low = split(jnp.concatenate(turned, axis=1))
        final = dot(dfts[3, 0], high) + dot(dfts[3, 1], high) + dot(dfts[3, 0], low)
        final = final.astype(jnp.bfloat16)
        for beam in range(PAIR):
            for section in range(2):
                message = (chunk * PAIR + beam) * 2 + section
                results[message, parity] = final[
                    section * SIDE : (section + 1) * SIDE, beam * SIDE : (beam + 1) * SIDE
                ]

        def send(index, carry):
            beam = index // 2
            section = lax.rem(index, 2)
            beam_id = target_beam(beam)
            message = chunk * (2 * PAIR) + index
            own = jnp.logical_and(beam_id == me, section == core)

            @pl.when(own)
            def _():
                pltpu.make_async_copy(
                    results.at[message, parity], gathered.at[parity, slot], own_sem.at[CHUNKS]
                ).start()

            @pl.when(jnp.logical_not(own))
            def _():
                pltpu.make_async_remote_copy(
                    src_ref=results.at[message, parity],
                    dst_ref=gathered.at[parity, slot],
                    send_sem=z_send,
                    recv_sem=z_recv,
                    device_id=(beam_id, section),
                    device_id_type=MESH,
                ).start()

            return carry

        lax.fori_loop(0, 2 * PAIR, send, 0)
        return carry

    lax.fori_loop(0, 2 * CHUNKS, do_half, 0)

    for chunk in range(1, CHUNKS):
        wait_x_sent(chunk)
    others = 2 * NZ * NY - 1
    pltpu.make_async_copy(
        results.at[0], gathered.at[:, slot], own_sem.at[CHUNKS]
    ).wait()
    pltpu.make_async_copy(results.at[pl.ds(0, others)], results.at[pl.ds(0, others)], z_send).wait()
    pltpu.make_async_copy(
        gathered.at[:, pl.ds(0, others)], gathered.at[:, pl.ds(0, others)], z_recv
    ).wait()


BLOCK = 8
PARTS = 4


def place_kernel(bounds, gathered, placed, rows, blank, in_sem, out_sem):
    me = lax.axis_index("sub")
    start, end = bounds[0, me], bounds[1, me]
    count = gathered.shape[0]
    part = count // PARTS
    loads = [
        pltpu.make_async_copy(
            gathered.at[pl.ds(p * part, part)], rows.at[pl.ds(p * part, part)], in_sem.at[p]
        )
        for p in range(PARTS)
    ]
    for load in loads:
        load.start()
    blank[...] = jnp.zeros_like(blank)

    def write_blank(block, carry):
        first = block * BLOCK

        @pl.when(jnp.logical_or(first + BLOCK <= start, first >= end))
        def _():
            pltpu.make_async_copy(blank, placed.at[pl.ds(first, BLOCK)], out_sem).start()

        return carry

    lax.fori_loop(0, 2 * count // BLOCK, write_blank, 0)

    def write_rows(block, carry):
        source = block * BLOCK
        for high in range(2):
            first = source + high * count
            whole = jnp.logical_and(first >= start, first + BLOCK <= end)
            some = jnp.logical_and(first < end, first + BLOCK > start)

            @pl.when(whole)
            def _():
                pltpu.make_async_copy(
                    rows.at[pl.ds(source, BLOCK)], placed.at[pl.ds(first, BLOCK)], out_sem
                ).start()

            @pl.when(jnp.logical_and(some, jnp.logical_not(whole)))
            def _():
                def one(index, carry):
                    row = first + index
                    live = jnp.logical_and(row >= start, row < end)

                    @pl.when(live)
                    def _():
                        pltpu.make_async_copy(
                            rows.at[pl.ds(source + index, 1)], placed.at[pl.ds(row, 1)], out_sem
                        ).start()

                    @pl.when(jnp.logical_not(live))
                    def _():
                        pltpu.make_async_copy(
                            blank.at[pl.ds(0, 1)], placed.at[pl.ds(row, 1)], out_sem
                        ).start()

                    return carry

                lax.fori_loop(0, BLOCK, one, 0)

        return carry

    blocks = part // BLOCK
    for p in range(PARTS):
        loads[p].wait()
        lax.fori_loop(p * blocks, (p + 1) * blocks, write_rows, 0)
    pltpu.make_async_copy(placed, placed, out_sem).wait()


def per_device(voltages, delay_table, delay_index, dm_table, dm_index, range_bounds):
    stations = voltages.shape[2]
    subbands = voltages.shape[0] * lax.axis_size("sub")
    frequency = 1.0 + (np.arange(subbands) + 0.5) / subbands
    cubes = (0.5 / (LENGTH * frequency**3)).astype(np.float32)
    dfts, planes = dft_tables()
    cosine_poly, sine_poly = turn_coefficients()
    vmem = pl.BlockSpec(memory_space=pltpu.VMEM)
    smem = pl.BlockSpec(memory_space=pltpu.SMEM)
    far = pl.BlockSpec(memory_space=pl.ANY)
    bounds = range_bounds.T
    gathered = pl.pallas_call(
        functools.partial(kernel, cosine_poly, sine_poly),
        out_shape=jax.ShapeDtypeStruct((2, NZ * NY * 2, SIDE, SIDE), jnp.bfloat16),
        in_specs=[smem] * 5 + [vmem] * 2 + [far] * 3,
        out_specs=far,
        scratch_shapes=[
            pltpu.VMEM((2, 2 * stations, HALF), jnp.bfloat16),
            pltpu.VMEM(dfts.shape, dfts.dtype),
            pltpu.VMEM(planes.shape, planes.dtype),
            pltpu.VMEM((2, CHUNKS * NX * 8, 4 * stations), jnp.bfloat16),
            pltpu.VMEM((2 * CHUNKS * NX, 16, PIECE), jnp.bfloat16),
            pltpu.VMEM((CHUNKS, 2 * NX, 16, PIECE), jnp.bfloat16),
            pltpu.VMEM((4 * SIDE, SIDE), jnp.float32),
            pltpu.VMEM((CHUNKS * PAIR * 2, 2, SIDE, SIDE), jnp.bfloat16),
            pltpu.SemaphoreType.DMA((CHUNKS,)),
            pltpu.SemaphoreType.DMA((2 * CHUNKS,)),
            pltpu.SemaphoreType.DMA,
            pltpu.SemaphoreType.DMA,
            pltpu.SemaphoreType.DMA((CHUNKS + 1,)),
            pltpu.SemaphoreType.DMA((3,)),
        ],
        compiler_params=pltpu.CompilerParams(
            collective_id=0, has_side_effects=True, vmem_limit_bytes=56 * 1024 * 1024
        ),
        name="beams",
    )(
        delay_table,
        dm_table,
        dm_index,
        bounds,
        jnp.asarray(cubes),
        delay_index.T,
        bounds,
        voltages.reshape(2, 2 * stations, HALF),
        jnp.asarray(dfts),
        jnp.asarray(planes),
    )

    rows = subbands // 2
    placed = pl.pallas_call(
        place_kernel,
        in_specs=[smem, far],
        out_specs=far,
        out_shape=jax.ShapeDtypeStruct((subbands, SIDE, SIDE), jnp.bfloat16),
        scratch_shapes=[
            pltpu.VMEM((rows, SIDE, SIDE), jnp.bfloat16),
            pltpu.VMEM((BLOCK, SIDE, SIDE), jnp.bfloat16),
            pltpu.SemaphoreType.DMA((PARTS,)),
            pltpu.SemaphoreType.DMA,
        ],
        compiler_params=pltpu.CompilerParams(vmem_limit_bytes=56 * 1024 * 1024),
        name="place",
    )(bounds, gathered.reshape(rows, SIDE, SIDE))
    placed = placed.reshape(subbands, SIDE // 2, 2, SIDE)
    return jnp.transpose(placed, (0, 2, 1, 3)).reshape(1, subbands, 2, HALF)


def solution(mesh):
    return jax.shard_map(
        per_device,
        mesh=mesh,
        in_specs=(P("sub", None, None, "section"), P(), P(), P(), P(), P()),
        out_specs=P("sub", None, None, "section"),
        check_vma=False,
    )
```

```python
import functools
import math

import jax
import jax.numpy as jnp
import numpy as np
from jax import lax
from jax.experimental import pallas as pl
from jax.experimental.pallas import tpu as pltpu
from jax.sharding import PartitionSpec as P

MESH = pl.DeviceIdType.MESH
NX, NZ, NY = 4, 8, 4
LENGTH = 16384
SIDE = 128
HALF = LENGTH // 2
PIECES = 4
PIECE = HALF // PIECES
PAIR = 2
CHUNKS = NZ * NY // PAIR
AHEAD = 2
LANES = 256


def chunk_offset(chunk):
    index = chunk // 2
    step = (index + 1) // 2
    return (NZ // 2 + step * (1 - 2 * (index % 2)) + NZ) % NZ


def split_table(table):
    high = table.astype(jnp.bfloat16)
    low = (table - high.astype(np.float64)).astype(jnp.bfloat16)
    return np.stack([high, low])


def dft_tables():
    index = np.arange(SIDE)
    angle = 2.0 * np.pi * (np.outer(index, index) % SIDE) / SIDE
    cosine, sine = np.cos(angle), np.sin(angle)
    first = np.block([[cosine, sine], [-sine, cosine]])
    first = first.reshape(2 * SIDE, 2, 2, 2, 2, PIECE // SIDE)
    first = first.transpose(0, 1, 4, 2, 3, 5).reshape(2 * SIDE, 2 * SIDE)
    second = np.block([[cosine, -sine], [sine, cosine]])
    third = np.block([[cosine, sine], [-sine, cosine]])
    fourth = np.empty((SIDE, 2, 2 * SIDE))
    fourth[:, 0] = np.concatenate([cosine, -sine], axis=1)
    fourth[:, 1] = np.concatenate([sine, cosine], axis=1)
    fourth = fourth.reshape(2 * SIDE, 2 * SIDE) / LENGTH
    dfts = np.stack([split_table(t) for t in (first, second, third, fourth)])
    twist = 2.0 * np.pi * np.outer(index, index) / LENGTH
    bins = index[:, None] + SIDE * np.where(index < SIDE // 2, index, index - SIDE)[None, :]
    planes = np.stack([np.cos(twist), np.sin(twist), (bins * bins).astype(np.float64)])
    return dfts, planes.astype(np.float32)


def turn_coefficients():
    grid = np.cos(np.pi * (np.arange(400) + 0.5) / 400) * 0.25 + 0.25
    x = np.sqrt(grid) * 0.5 / np.sqrt(0.5)
    square = x * x
    cosine = np.polynomial.chebyshev.Chebyshev.fit(square, np.cos(2 * np.pi * x), 6, domain=[0, 0.25])
    sine = np.polynomial.chebyshev.Chebyshev.fit(
        square, np.sin(2 * np.pi * x) / x, 6, domain=[0, 0.25]
    )
    power = np.polynomial.Polynomial
    return (
        [float(v) for v in cosine.convert(kind=power).coef],
        [float(v) for v in sine.convert(kind=power).coef],
    )


def horner(coefficients, x):
    total = coefficients[-1]
    for value in coefficients[-2::-1]:
        total = total * x + value
    return total


def split(value):
    high = value.astype(jnp.bfloat16)
    return high, (value - high.astype(jnp.float32)).astype(jnp.bfloat16)


def dot(left, right):
    return jnp.dot(left, right, preferred_element_type=jnp.float32)


def turn_cos_sin(turns, cosine_poly, sine_poly):
    turns = turns - jnp.round(turns)
    square = turns * turns
    return horner(cosine_poly, square), horner(sine_poly, square) * turns


def kernel(
    cosine_poly,
    sine_poly,
    delay_table,
    dm_table,
    dm_index,
    bounds_scalar,
    cubes,
    delay_index,
    bounds,
    voltages_far,
    dfts_far,
    planes_far,
    gathered,
    voltages,
    dfts,
    planes,
    weights,
    formed,
    arrived,
    grid,
    results,
    x_send,
    x_recv,
    z_send,
    z_recv,
    own_sem,
    load_sem,
):
    loads = [
        pltpu.make_async_copy(far, near, load_sem.at[index])
        for index, (far, near) in enumerate(
            [(voltages_far, voltages), (dfts_far, dfts), (planes_far, planes)]
        )
    ]
    for load in loads:
        load.start()

    me = lax.axis_index("sub")
    core = lax.axis_index("section")
    my_x = me // (NZ * NY)
    my_z = lax.rem(me // NY, NZ)
    my_y = lax.rem(me, NY)
    plane_start = my_x * (NZ * NY)

    barrier = pltpu.get_barrier_semaphore()

    def x_partner(step):
        other_x = lax.rem(my_x - step // 2 + NX, NX)
        other_core = lax.rem(core + lax.rem(step, 2), 2)
        return other_x, other_core

    def greet_x(step, carry):
        other_x, other_core = x_partner(step)
        pl.semaphore_signal(
            barrier, inc=1, device_id=((other_x * NZ + my_z) * NY + my_y, other_core), device_id_type=MESH
        )
        return carry

    def greet_plane(step, carry):
        other = lax.rem(my_z * NY + my_y + step // 2, NZ * NY)
        other_core = lax.rem(core + lax.rem(step, 2), 2)
        pl.semaphore_signal(
            barrier, inc=1, device_id=(plane_start + other, other_core), device_id_type=MESH
        )
        return carry

    lax.fori_loop(2, 2 * NX, greet_x, 0, unroll=True)
    lax.fori_loop(1, 2 * NZ * NY, greet_plane, 0, unroll=9)

    beams = NX * NZ * NY
    stations = delay_index.shape[0]
    subbands = 2 * beams

    entries = delay_index[...]

    def look_up(entry, total):
        return jnp.where(entries == entry, delay_table[entry], total)

    delays = lax.fori_loop(
        0, delay_table.shape[0], look_up, jnp.zeros((stations, beams), jnp.float32), unroll=8
    )
    scaling = 1.0 / math.sqrt(stations)
    sources = []
    for local in range(2):
        subband = 2 * me + local
        freq = 1.0 + (subband.astype(jnp.float32) + 0.5) * (1.0 / subbands)
        cosine, sine = turn_cos_sin(delays * freq, cosine_poly, sine_poly)
        live = jnp.logical_and(bounds[0:1, :] <= subband, bounds[1:2, :] > subband)
        cosine = jnp.where(live, cosine * scaling, 0.0)
        sine = jnp.where(live, sine * scaling, 0.0)
        both = jnp.concatenate(
            [
                jnp.concatenate([cosine, -sine], axis=1),
                jnp.concatenate([sine, cosine], axis=1),
            ],
            axis=0,
        )
        sources.append(jnp.concatenate([both, both], axis=0).astype(jnp.bfloat16))

    def weigh(first, count):
        height = count * NX * 8
        row = first * NX * 8 + lax.broadcasted_iota(jnp.int32, (height, 1), 0)
        row_chunk = row >> 5
        row_index = row_chunk >> 1
        row_offset = NZ // 2 + ((row_index + 1) >> 1) * (1 - 2 * (row_index & 1))
        row_pair = (row >> 1) & 1
        row_z = (my_z + (1 - 2 * row_pair) * row_offset + 2 * NZ) & (NZ - 1)
        row_y = (my_y + PAIR * row_pair + (row_chunk & 1)) & (NY - 1)
        row_beam = ((row >> 3) & (NX - 1)) * (NZ * NY) + row_z * NY + row_y
        column = lax.broadcasted_iota(jnp.int32, (height, 2 * beams), 1)
        chosen = jnp.where(column == (row & 1) * beams + row_beam, 1.0, 0.0).astype(jnp.bfloat16)
        lane = lax.broadcasted_iota(jnp.int32, (height, 4 * stations), 1)
        same = ((row >> 2) & 1) == jnp.where(lane >= 2 * stations, 1, 0)
        for local in range(2):
            placed = lax.dot_general(
                chosen, sources[local], (((1,), (1,)), ((), ())), preferred_element_type=jnp.float32
            )
            weights[local, first * NX * 8 : (first + count) * NX * 8] = jnp.where(
                same, placed, 0.0
            ).astype(jnp.bfloat16)

    weigh(0, 1)
    tiles = PIECE // LANES

    def form(first, count, step, carry):
        local = step // tiles
        start = lax.rem(step, tiles) * LANES
        parts = []
        for couple in range(2):
            blocks = [
                voltages[
                    local, :, pl.ds(pl.multiple_of((couple * 2 + piece) * PIECE + start, LANES), LANES)
                ]
                for piece in range(2)
            ]
            product = dot(
                weights[local, first * NX * 8 : (first + count) * NX * 8],
                jnp.concatenate(blocks, axis=0),
            )
            parts.append(product.reshape(count * NX, 8, LANES))
        both = jnp.concatenate(parts, axis=1).astype(jnp.bfloat16)
        formed[
            pl.ds(local * (CHUNKS * NX) + first * NX, count * NX),
            :,
            pl.ds(pl.multiple_of(start, LANES), LANES),
        ] = both
        return carry

    loads[0].wait()
    lax.fori_loop(0, 2 * tiles, functools.partial(form, 0, 1), 0)

    pl.semaphore_wait(barrier, 2 * NX - 2 + 2 * NZ * NY - 1)

    def x_copy(chunk, step):
        other_x, other_core = x_partner(step)
        group = lax.rem(step // 2, 2)
        place = group * NX + (step // NX) * 2 + lax.rem(step, 2)
        return pltpu.make_async_remote_copy(
            src_ref=formed.at[(other_core * CHUNKS + chunk) * NX + other_x],
            dst_ref=arrived.at[chunk, place],
            send_sem=x_send.at[chunk],
            recv_sem=x_recv.at[chunk * 2 + group],
            device_id=((other_x * NZ + my_z) * NY + my_y, other_core),
            device_id_type=MESH,
        )

    def own_copy(chunk):
        return pltpu.make_async_copy(
            formed.at[(core * CHUNKS + chunk) * NX + my_x], arrived.at[chunk, 0], own_sem.at[chunk]
        )

    def start_x(chunk):
        def one(step, carry):
            x_copy(chunk, step).start()
            return carry

        lax.fori_loop(NX, NX + 2, one, 0)
        x_copy(chunk, 1).start()
        own_copy(chunk).start()
        lax.fori_loop(2, NX, one, 0)
        lax.fori_loop(NX + 2, 2 * NX, one, 0)

    def wait_x_sent(chunk):
        pltpu.make_async_copy(
            formed.at[pl.ds(0, 2 * NX - 1)], formed.at[pl.ds(0, 2 * NX - 1)], x_send.at[chunk]
        ).wait()

    start_x(0)
    weigh(1, CHUNKS - 1)
    lax.fori_loop(0, 2 * tiles, functools.partial(form, 1, CHUNKS - 1), 0)
    for load in loads[1:]:
        load.wait()
    wait_x_sent(0)
    start_x(1)

    slot = (my_z * NY + my_y) * 2 + core

    def do_half(step, carry):
        chunk = step // 2
        group = lax.rem(step, 2)

        @pl.when(group == 0)
        def _():
            near = arrived.at[chunk, pl.ds(1, NX - 1)]
            pltpu.make_async_copy(near, near, x_recv.at[step]).wait()
            own_copy(chunk).wait()

            @pl.when(chunk < CHUNKS - AHEAD)
            def _():
                start_x(chunk + AHEAD)

        @pl.when(group == 1)
        def _():
            far = arrived.at[chunk, pl.ds(NX, NX)]
            pltpu.make_async_copy(far, far, x_recv.at[step]).wait()

        offset = chunk_offset(chunk)
        parity = lax.rem(my_x + group, 2)

        def fold(other, carry):
            half = lax.rem(core + other, 2)

            def lane_tile(index, carry):
                lanes = pl.ds(pl.multiple_of(index * SIDE, SIDE), SIDE)
                near = arrived[chunk, group * NX + other, :, lanes].astype(jnp.float32)
                far = arrived[chunk, group * NX + 2 + other, :, lanes].astype(jnp.float32)
                total = near + far
                row = half * (SIDE // 4) + index
                grid[pl.ds(row, 8, stride=SIDE // 2), :] = total[:8]
                grid[pl.ds(row + SIDE // 8, 8, stride=SIDE // 2), :] = total[8:]
                return carry

            lax.fori_loop(0, PIECE // SIDE, lane_tile, 0, unroll=4)
            return carry

        lax.fori_loop(0, 2, fold, 0)

        def target_beam(beam):
            other_z = lax.rem(my_z + (1 - 2 * beam) * offset + NZ, NZ)
            other_y = lax.rem(my_y + PAIR * beam + lax.rem(chunk, 2), NY)
            return plane_start + other_z * NY + other_y

        series = []
        for beam in range(PAIR):
            pieces = [
                grid[pl.ds((piece * 4 + beam * 2 + part) * (SIDE // 2), SIDE // 2), :]
                for part in range(2)
                for piece in range(2)
            ]
            series.append(jnp.concatenate(pieces, axis=0))
        series = jnp.concatenate(series, axis=1).astype(jnp.bfloat16)
        low_row = parity * (subbands // 4) + 2 * (my_z * NY + my_y) + core
        high_row = low_row + subbands // 2
        stage = dot(dfts[0, 0], series) + dot(dfts[0, 1], series)
        cosine, sine = planes[0], planes[1]
        turned = []
        for beam in range(PAIR):
            lanes = slice(beam * SIDE, (beam + 1) * SIDE)
            real, imag = stage[:SIDE, lanes], stage[SIDE:, lanes]
            turned.append(
                jnp.concatenate([real * cosine + imag * sine, imag * cosine - real * sine], axis=1)
            )
        high, low = split(jnp.concatenate(turned, axis=0))
        stage = dot(high, dfts[1, 0]) + dot(high, dfts[1, 1]) + dot(low, dfts[1, 0])
        turned = []
        for beam in range(PAIR):
            rows_of = slice(beam * SIDE, (beam + 1) * SIDE)
            real, imag = stage[rows_of, :SIDE], stage[rows_of, SIDE:]
            beam_id = target_beam(beam)
            is_high = jnp.logical_and(
                bounds_scalar[0, beam_id] <= high_row, bounds_scalar[1, beam_id] > high_row
            )
            strength = dm_table[dm_index[beam_id]]
            dispersion = strength * cubes[jnp.where(is_high, high_row, low_row)]
            chirp_cos, chirp_sin = turn_cos_sin(dispersion * planes[2], cosine_poly, sine_poly)
            turned.append(
                jnp.concatenate(
                    [real * chirp_cos - imag * chirp_sin, real * chirp_sin + imag * chirp_cos], axis=1
                )
            )
        high, low = split(jnp.concatenate(turned, axis=0))
        stage = dot(high, dfts[2, 0]) + dot(high, dfts[2, 1]) + dot(low, dfts[2, 0])
        turned = []
        for beam in range(PAIR):
            rows_of = slice(beam * SIDE, (beam + 1) * SIDE)
            real, imag = stage[rows_of, :SIDE], stage[rows_of, SIDE:]
            turned.append(
                jnp.concatenate([real * cosine - imag * sine, real * sine + imag * cosine], axis=0)
            )
        high, low = split(jnp.concatenate(turned, axis=1))
        final = dot(dfts[3, 0], high) + dot(dfts[3, 1], high) + dot(dfts[3, 0], low)
        final = final.astype(jnp.bfloat16)
        for beam in range(PAIR):
            for section in range(2):
                message = (chunk * PAIR + beam) * 2 + section
                results[message, parity] = final[
                    section * SIDE : (section + 1) * SIDE, beam * SIDE : (beam + 1) * SIDE
                ]

        def send(index, carry):
            beam = index // 2
            section = lax.rem(index, 2)
            beam_id = target_beam(beam)
            message = chunk * (2 * PAIR) + index
            own = jnp.logical_and(beam_id == me, section == core)

            @pl.when(own)
            def _():
                pltpu.make_async_copy(
                    results.at[message, parity], gathered.at[parity, slot], own_sem.at[CHUNKS]
                ).start()

            @pl.when(jnp.logical_not(own))
            def _():
                pltpu.make_async_remote_copy(
                    src_ref=results.at[message, parity],
                    dst_ref=gathered.at[parity, slot],
                    send_sem=z_send,
                    recv_sem=z_recv,
                    device_id=(beam_id, section),
                    device_id_type=MESH,
                ).start()

            return carry

        lax.fori_loop(0, 2 * PAIR, send, 0)
        return carry

    lax.fori_loop(0, 2 * CHUNKS, do_half, 0)

    for chunk in range(1, CHUNKS):
        wait_x_sent(chunk)
    others = 2 * NZ * NY - 1
    pltpu.make_async_copy(
        results.at[0], gathered.at[:, slot], own_sem.at[CHUNKS]
    ).wait()
    pltpu.make_async_copy(results.at[pl.ds(0, others)], results.at[pl.ds(0, others)], z_send).wait()
    pltpu.make_async_copy(
        gathered.at[:, pl.ds(0, others)], gathered.at[:, pl.ds(0, others)], z_recv
    ).wait()


BLOCK = 8


def place_kernel(bounds, gathered, placed, blank, out_sem):
    me = lax.axis_index("sub")
    start, end = bounds[0, me], bounds[1, me]
    count = gathered.shape[0]
    blank[...] = jnp.zeros_like(blank)

    def write_blank(block, carry):
        first = block * BLOCK

        @pl.when(jnp.logical_or(first + BLOCK <= start, first >= end))
        def _():
            pltpu.make_async_copy(blank, placed.at[pl.ds(first, BLOCK)], out_sem).start()

        return carry

    lax.fori_loop(0, 2 * count // BLOCK, write_blank, 0)

    def write_rows(block, carry):
        source = block * BLOCK
        for high in range(2):
            first = source + high * count
            whole = jnp.logical_and(first >= start, first + BLOCK <= end)
            some = jnp.logical_and(first < end, first + BLOCK > start)

            @pl.when(whole)
            def _():
                pltpu.make_async_copy(
                    gathered.at[pl.ds(source, BLOCK)], placed.at[pl.ds(first, BLOCK)], out_sem
                ).start()

            @pl.when(jnp.logical_and(some, jnp.logical_not(whole)))
            def _():
                def one(index, carry):
                    row = first + index
                    live = jnp.logical_and(row >= start, row < end)

                    @pl.when(live)
                    def _():
                        pltpu.make_async_copy(
                            gathered.at[pl.ds(source + index, 1)], placed.at[pl.ds(row, 1)], out_sem
                        ).start()

                    @pl.when(jnp.logical_not(live))
                    def _():
                        pltpu.make_async_copy(
                            blank.at[pl.ds(0, 1)], placed.at[pl.ds(row, 1)], out_sem
                        ).start()

                    return carry

                lax.fori_loop(0, BLOCK, one, 0)

        return carry

    lax.fori_loop(0, count // BLOCK, write_rows, 0)
    pltpu.make_async_copy(placed, placed, out_sem).wait()


def per_device(voltages, delay_table, delay_index, dm_table, dm_index, range_bounds):
    stations = voltages.shape[2]
    subbands = voltages.shape[0] * lax.axis_size("sub")
    frequency = 1.0 + (np.arange(subbands) + 0.5) / subbands
    cubes = (0.5 / (LENGTH * frequency**3)).astype(np.float32)
    dfts, planes = dft_tables()
    cosine_poly, sine_poly = turn_coefficients()
    vmem = pl.BlockSpec(memory_space=pltpu.VMEM)
    smem = pl.BlockSpec(memory_space=pltpu.SMEM)
    far = pl.BlockSpec(memory_space=pl.ANY)
    bounds = range_bounds.T
    gathered = pl.pallas_call(
        functools.partial(kernel, cosine_poly, sine_poly),
        out_shape=pltpu.VMEM((2, NZ * NY * 2, SIDE, SIDE), jnp.bfloat16),
        in_specs=[smem] * 5 + [vmem] * 2 + [far] * 3,
        out_specs=far,
        scratch_shapes=[
            pltpu.VMEM((2, 2 * stations, HALF), jnp.bfloat16),
            pltpu.VMEM(dfts.shape, dfts.dtype),
            pltpu.VMEM(planes.shape, planes.dtype),
            pltpu.VMEM((2, CHUNKS * NX * 8, 4 * stations), jnp.bfloat16),
            pltpu.VMEM((2 * CHUNKS * NX, 16, PIECE), jnp.bfloat16),
            pltpu.VMEM((CHUNKS, 2 * NX, 16, PIECE), jnp.bfloat16),
            pltpu.VMEM((4 * SIDE, SIDE), jnp.float32),
            pltpu.VMEM((CHUNKS * PAIR * 2, 2, SIDE, SIDE), jnp.bfloat16),
            pltpu.SemaphoreType.DMA((CHUNKS,)),
            pltpu.SemaphoreType.DMA((2 * CHUNKS,)),
            pltpu.SemaphoreType.DMA,
            pltpu.SemaphoreType.DMA,
            pltpu.SemaphoreType.DMA((CHUNKS + 1,)),
            pltpu.SemaphoreType.DMA((3,)),
        ],
        compiler_params=pltpu.CompilerParams(
            collective_id=0, has_side_effects=True, vmem_limit_bytes=54 * 1024 * 1024
        ),
        name="beams",
    )(
        delay_table,
        dm_table,
        dm_index,
        bounds,
        jnp.asarray(cubes),
        delay_index.T,
        bounds,
        voltages.reshape(2, 2 * stations, HALF),
        jnp.asarray(dfts),
        jnp.asarray(planes),
    )

    rows = subbands // 2
    placed = pl.pallas_call(
        place_kernel,
        in_specs=[smem, far],
        out_specs=far,
        out_shape=jax.ShapeDtypeStruct((subbands, SIDE, SIDE), jnp.bfloat16),
        scratch_shapes=[
            pltpu.VMEM((BLOCK, SIDE, SIDE), jnp.bfloat16),
            pltpu.SemaphoreType.DMA,
        ],
        compiler_params=pltpu.CompilerParams(vmem_limit_bytes=16 * 1024 * 1024),
        name="place",
    )(bounds, gathered.reshape(rows, SIDE, SIDE))
    placed = placed.reshape(subbands, SIDE // 2, 2, SIDE)
    return jnp.transpose(placed, (0, 2, 1, 3)).reshape(1, subbands, 2, HALF)


def solution(mesh):
    return jax.shard_map(
        per_device,
        mesh=mesh,
        in_specs=(P("sub", None, None, "section"), P(), P(), P(), P(), P()),
        out_specs=P("sub", None, None, "section"),
        check_vma=False,
    )
```
